32 devices in a mesh: sec: 4 (over x, core), op: 8 (over z, y).
Axes of the slice: x: 2, y: 2, z: 4, core: 2. Of those that a mesh axis runs over, the one named last changes fastest.
Arguments:
- wavefunction: bfloat16 [4, 768, 768], P('sec', 'op'), may hold values from -6 to 6
- left_ops: bfloat16 [4, 24, 768, 768], P('sec', 'op'), may hold values from -0.046875 to 0.046875
- right_ops: bfloat16 [4, 24, 768, 768], P('sec', 'op'), may hold values from -0.21875 to 0.21875
- diagonal: float32 [4, 768, 768], P('sec', 'op'), may hold values from 0.15 to 10.2
- sector_sizes: int32 [4], P('sec'), may hold values from 192 to 768
- partner: int32 [4], replicated, may hold values from 0 to 3, as said below
Outputs:
- updated: float32 [4, 768, 768], P('sec', 'op')
- residual: float32 [4, 768, 768], P('sec', 'op')
The draws below stay inside these ranges and needn't reach their ends.
Inputs may be any that keep to these rules, and one draw needn't show every extreme that they name: `partner`: each sector is named exactly once.
All inputs are finite; a program needn't handle non-finite values.
Results may differ from the reference program's by a relative error of at most 0.0017.
Values may be sent and summed in bfloat16 or wider, within the bound.
A program may use at most 64 MiB of HBM per device.

```python
import jax
import jax.numpy as jnp
from jax import lax

B = 768
SECTORS = 4
TERMS = 24


def draw_diagonal(key, part):
    noise_key = jax.random.fold_in(key, 7)
    sector_pos = jnp.arange(SECTORS, dtype=jnp.float32) / float(max(SECTORS - 1, 1))
    row_pos = jnp.arange(B, dtype=jnp.float32) / float(max(B - 1, 1))
    level = 0.5 + 1.5 * sector_pos
    rising = 1.0 + 2.0 * row_pos
    noise = jax.random.uniform(noise_key, (SECTORS, B, B), jnp.float32, 0.6, 1.4)
    return level[:, None, None] * rising[None, :, None] * noise


def draw_partner(key, part):
    order_key = jax.random.fold_in(key, 11)
    shuffled = jax.random.permutation(order_key, SECTORS).astype(jnp.int32)
    middle = SECTORS // 2
    first_value = shuffled[0]
    places = jnp.arange(SECTORS, dtype=jnp.int32)
    swapped = jnp.where(shuffled == middle, first_value, shuffled)
    return jnp.where(places == 0, jnp.int32(middle), swapped).astype(jnp.int32)


def touch_ends(drawn, stream_key, smallest, largest):
    shape = drawn.shape
    place = [jax.random.randint(jax.random.fold_in(stream_key, axis), (), 0, shape[axis]) for axis in range(len(shape))]
    drawn = drawn.at[tuple(place)].set(smallest)
    longest = shape.index(max(shape))
    place[longest] = (place[longest] + 1) % shape[longest]
    return drawn.at[tuple(place)].set(largest)


def level_of(key, dims, shards, low, top_value):
    def one(position, shards_of):
        draws = jax.random.uniform(jax.random.fold_in(jax.random.fold_in(key, 6), position), (shards_of,), jnp.float32, low / len(shards), top_value / len(shards))
        return jnp.repeat(jnp.exp(draws), dims[position] // shards_of).reshape((-1,) + (1,) * (len(dims) - position - 1))

    level = one(*shards[0])
    for cut in shards[1:]:
        level = level * one(*cut)
    return level


def scatter_about(stream_key, dims, deviation, limit, shards=(), kind=jnp.bfloat16):
    gain = level_of(stream_key, dims, shards, -0.22, 0.18) if shards else 1.0
    array = jax.random.normal(stream_key, dims, jnp.float32) * deviation * gain
    return jnp.minimum(jnp.maximum(array, -limit), limit).astype(kind)


def setup_inputs(seed: int = 0) -> dict:
    seeds = jax.random.split(jax.random.key(seed), 7)
    return {
        "wavefunction": scatter_about(seeds[0], (SECTORS, B, B), 1.0, 6.0, ((0, 4), (1, 8))),
        "left_ops": scatter_about(seeds[1], (SECTORS, TERMS, B, B), (B * TERMS) ** -0.5, 0.046875, ((0, 4), (1, 8))),
        "right_ops": scatter_about(seeds[2], (SECTORS, TERMS, B, B), B ** -0.5, 0.21875, ((0, 4), (1, 8))),
        "diagonal": draw_diagonal(jax.random.fold_in(seeds[6], 71), 0),
        "sector_sizes": touch_ends(jax.random.randint(seeds[4], (SECTORS,), B // 4, B + 1), jax.random.fold_in(seeds[4], 1), B // 4, B).astype(jnp.int32),
        "partner": draw_partner(jax.random.fold_in(seeds[6], 71), 0),
    }


def reference(wavefunction, left_ops, right_ops, diagonal, sector_sizes, partner):
    positions = jnp.arange(B, dtype=jnp.int32)
    live_mask = (positions[None, :, None] < sector_sizes[:, None, None]) & (positions[None, None, :] < sector_sizes[:, None, None])
    live = jnp.where(live_mask, wavefunction, jnp.zeros_like(wavefunction))

    def sector_step(carried, sector):
        direct_all, adjoint_all = carried
        other = partner[sector]
        left_float = left_ops[sector].astype(jnp.float32)
        right_float = right_ops[sector].astype(jnp.float32)
        forward = jnp.einsum('kab,bc->kac', left_float, live[other].astype(jnp.float32)).astype(jnp.bfloat16)
        direct_term = jnp.einsum('kac,kdc->ad', forward.astype(jnp.float32), right_float)
        backward = jnp.einsum('kba,bc->kac', left_float, live[sector].astype(jnp.float32)).astype(jnp.bfloat16)
        adjoint_term = jnp.einsum('kac,kcd->ad', backward.astype(jnp.float32), right_float)
        direct_all = direct_all.at[sector].set(direct_term)
        adjoint_all = adjoint_all.at[other].add(adjoint_term)
        return (direct_all, adjoint_all), 0

    zero_blocks = jnp.zeros((SECTORS, B, B), jnp.float32)
    (direct_all, adjoint_all), _ = lax.scan(sector_step, (zero_blocks, zero_blocks), jnp.arange(SECTORS, dtype=jnp.int32))
    wave_float = live.astype(jnp.float32)
    sigma = jnp.where(live_mask, direct_all + adjoint_all + diagonal * wave_float, jnp.zeros_like(direct_all))
    energy = jnp.sum(wave_float * sigma) / jnp.sum(wave_float * wave_float)
    residual = sigma - energy * wave_float
    updated = wave_float - residual / jnp.maximum(jnp.abs(diagonal - energy), 1.0)
    return updated, residual
```

```python
import functools

import jax
import jax.numpy as jnp
from jax import lax
from jax.experimental import pallas as pl
from jax.experimental.pallas import tpu as pltpu
from jax.sharding import PartitionSpec as P

MESH = pl.DeviceIdType.MESH
F32 = jnp.float32
BF16 = jnp.bfloat16
PAIR = 2


def nt_dot(a, b):
    return lax.dot_general(a, b, (((1,), (1,)), ((), ())), preferred_element_type=F32)


def nn_dot(a, b):
    return lax.dot_general(a, b, (((1,), (0,)), ((), ())), preferred_element_type=F32)


def fold_sum(value):
    rows, width = value.shape
    part = jnp.sum(value.reshape(rows // 8, 8, width), axis=0)
    total = part[:, :128]
    for start in range(128, width, 128):
        total = total + part[:, start : start + 128]
    return total


def kernel(
    sectors, ops,
    partner_ref, sizes_ref, wave_ref, diag_ref, left_hbm, right_hbm,
    sigma_ref, energy_ref,
    left, right, left_t, own, other, own_full, other_full, by_sector, acc,
    adj_keep, adj_ys, adj_yr, adj_zs, adj_zr, routed,
    dir_keep, dir_ys, dir_yr, dir_zs, dir_zr,
    scalars, scalar_y, scalar_z, scalar_s,
    load_sem,
    own_send, own_recv, other_send, other_recv,
    sec_send, sec_recv, route_send, route_recv,
    adj_send, adj_recv, dir_send, dir_recv, sc_send, sc_recv,
):
    far_count = ops // PAIR
    me_sec = lax.axis_index("sec")
    me_op = lax.axis_index("op")
    far, near = me_op // PAIR, lax.rem(me_op, PAIR)
    rows, width = wave_ref.shape[1:]
    terms = left.shape[0]

    def far_at(step):
        return lax.rem(far + step + far_count, far_count)

    def sec_at(step):
        return lax.rem(me_sec + step + sectors, sectors)

    near_peer = (me_sec, far * PAIR + (1 - near))

    def far_peer(step):
        return (me_sec, far_at(step) * PAIR + near)

    def sec_peer(step):
        return (sec_at(step), me_op)

    def remote(src, dst, send, recv, device):
        return pltpu.make_async_remote_copy(
            src_ref=src, dst_ref=dst, send_sem=send, recv_sem=recv, device_id=device, device_id_type=MESH
        )

    started = []

    def send(*args):
        copy = remote(*args)
        copy.start()
        started.append(copy)

    load_left = pltpu.make_async_copy(left_hbm.at[0], left, load_sem.at[0])
    load_right = pltpu.make_async_copy(right_hbm.at[0], right, load_sem.at[1])
    load_left.start()
    load_right.start()

    barrier = pltpu.get_barrier_semaphore()
    peers = [near_peer]
    peers += [far_peer(step) for step in range(1, far_count)]
    peers += [sec_peer(step) for step in range(1, sectors)]
    for peer in peers:
        pl.semaphore_signal(barrier, inc=1, device_id=peer, device_id_type=MESH)

    size = sizes_ref[0]
    row_index = me_op * rows + lax.broadcasted_iota(jnp.int32, (rows, width), 0)
    col_index = lax.broadcasted_iota(jnp.int32, (rows, width), 1)
    live_mask = (row_index < size) & (col_index < size)
    wave = jnp.where(live_mask, wave_ref[0].astype(F32), 0.0)
    live = wave.astype(BF16)
    own[me_op] = live
    by_sector[me_sec] = live
    pl.semaphore_wait(barrier, len(peers))

    def gather_first(buf, sends, recvs):
        block = buf.at[me_op]
        for step in range(far_count - 1, 0, -1):
            send(block, block, sends.at[step], recvs.at[step], far_peer(step))
        send(block, block, sends.at[far_count], recvs.at[far_count], near_peer)

    def gather_pass(buf, sends, recvs, step):
        block = buf.at[far_at(-step) * PAIR + near]
        remote(block, block, sends.at[step], recvs.at[step], near_peer).wait_recv()
        send(block, block, sends.at[far_count + step], recvs.at[far_count + step], near_peer)

    def gather_last(buf, sends, recvs, full):
        for step in range(far_count):
            block = buf.at[far_at(-step) * PAIR + (1 - near)]
            remote(block, block, sends.at[far_count + step], recvs.at[far_count + step], near_peer).wait_recv()
        if rows % 16 == 0:
            full[...] = buf[...].reshape(ops * rows, width)
        else:
            full[...] = buf[...].astype(F32).reshape(ops * rows, width).astype(BF16)

    for step in range(1, sectors):
        send(by_sector.at[me_sec], by_sector.at[me_sec], sec_send.at[step], sec_recv.at[step], sec_peer(step))
    gather_first(own, own_send, own_recv)

    load_left.wait()

    def turn(term, carry):
        left_t[term] = left[term].T
        return carry

    lax.fori_loop(0, terms, turn, 0)

    for step in range(1, sectors):
        block = by_sector.at[sec_at(-step)]
        remote(block, block, sec_send.at[step], sec_recv.at[step], near_peer).wait_recv()
    other[me_op] = by_sector[partner_ref[me_sec]]
    gather_first(other, other_send, other_recv)

    for step in range(1, far_count):
        gather_pass(own, own_send, own_recv, step)
    gather_last(own, own_send, own_recv, own_full)
    load_right.wait()

    order = list(range(1, far_count)) + [0]
    half = (far_count + 1) // 2
    groups = [order[:half], order[half:]]
    span = PAIR * rows

    def products(group, left_side, middle, last_dot, weight, keep, ys, yr, sends, recvs):
        places = [pl.ds(pl.multiple_of(far_at(step) * span, span), span) for step in group]
        count = len(group) * span
        total = acc.at[pl.ds(0, count)]

        def one(term, carry):
            lhs = jnp.concatenate([left_side[term, place, :] for place in places], axis=0)
            inner = nn_dot(lhs, middle[...]).astype(BF16)
            out = last_dot(inner, right[term])

            @pl.when(term == 0)
            def _():
                total[...] = out

            @pl.when(term > 0)
            def _():
                total[...] += out

            return carry

        lax.fori_loop(0, terms, one, 0)
        for at, (step, place) in enumerate(zip(group, places)):
            first = acc[at * span : at * span + rows, :]
            second = acc[at * span + rows : (at + 1) * span, :]
            keep[step] = jnp.where(near == 0, first, second)
            ys[step] = jnp.where(near == 0, second, first).astype(BF16)
            send(ys.at[step], yr.at[step], sends.at[step], recvs.at[step], near_peer)
        for at, (step, place) in enumerate(zip(group, places)):
            whole = acc[at * span : (at + 1) * span, :]
            scalars[0] += fold_sum(whole * weight[place, :].astype(F32))

    def pass_on(step, keep, yr, zs, zr, sends, recvs):
        remote(yr.at[step], yr.at[step], sends.at[step], recvs.at[step], near_peer).wait_recv()
        summed = keep[step] + yr[step].astype(F32)
        if step == 0:
            keep[0] = summed
        else:
            zs[step] = summed.astype(BF16)
            at = far_count + step
            send(zs.at[step], zr.at[step], sends.at[at], recvs.at[at], far_peer(step))

    def finish(keep, zr, sends, recvs):
        total = keep[0]
        for step in range(1, far_count):
            at = far_count + step
            remote(zr.at[step], zr.at[step], sends.at[at], recvs.at[at], near_peer).wait_recv()
            total = total + zr[step].astype(F32)
        return total

    diag = diag_ref[0]
    scalars[0] = fold_sum(diag * wave * wave)
    scalars[1] = fold_sum(wave * wave)

    def adjoint(group, first):
        places = [pl.ds(pl.multiple_of(far_at(step) * span, span), span) for step in group]
        total = acc.at[pl.ds(first * span, len(group) * span)]

        def one(term, carry):
            lhs = jnp.concatenate([left_t[term, place, :] for place in places], axis=0)
            inner = nn_dot(lhs, own_full[...]).astype(BF16)
            out = nn_dot(inner, right[term])

            @pl.when(term == 0)
            def _():
                total[...] = out

            @pl.when(term > 0)
            def _():
                total[...] += out

            return carry

        lax.fori_loop(0, terms, one, 0)
        for at, step in enumerate(group):
            base = (first + at) * span
            one_half = acc[base : base + rows, :]
            two_half = acc[base + rows : base + span, :]
            adj_keep[step] = jnp.where(near == 0, one_half, two_half)
            adj_ys[step] = jnp.where(near == 0, two_half, one_half).astype(BF16)
            send(adj_ys.at[step], adj_yr.at[step], adj_send.at[step], adj_recv.at[step], near_peer)

    adjoint(groups[0], 0)
    for step in range(1, far_count):
        gather_pass(other, other_send, other_recv, step)
    adjoint(groups[1], len(groups[0]))
    gather_last(other, other_send, other_recv, other_full)
    for at, step in enumerate(order):
        place = pl.ds(pl.multiple_of(far_at(step) * span, span), span)
        scalars[0] += fold_sum(acc[at * span : (at + 1) * span, :] * other_full[place, :].astype(F32))
    for step in groups[0]:
        pass_on(step, adj_keep, adj_yr, adj_zs, adj_zr, adj_send, adj_recv)

    products(groups[0], left, other_full, nt_dot, own_full, dir_keep, dir_ys, dir_yr, dir_send, dir_recv)
    for step in groups[1]:
        pass_on(step, adj_keep, adj_yr, adj_zs, adj_zr, adj_send, adj_recv)
    products(groups[1], left, other_full, nt_dot, own_full, dir_keep, dir_ys, dir_yr, dir_send, dir_recv)

    send(scalars, scalar_y, sc_send.at[0], sc_recv.at[0], near_peer)
    for step in order:
        pass_on(step, dir_keep, dir_yr, dir_zs, dir_zr, dir_send, dir_recv)
    remote(scalar_y, scalar_y, sc_send.at[0], sc_recv.at[0], near_peer).wait_recv()
    scalar_z[0] = scalars[...] + scalar_y[...]
    for step in range(1, far_count):
        send(scalar_z.at[0], scalar_z.at[step], sc_send.at[step], sc_recv.at[step], far_peer(step))

    routed[me_sec] = finish(adj_keep, adj_zr, adj_send, adj_recv)
    for step in range(1, sectors):
        send(routed.at[me_sec], routed.at[me_sec], route_send.at[step], route_recv.at[step], sec_peer(step))

    inner_sum = scalar_z[0]
    for step in range(1, far_count):
        remote(scalar_z.at[step], scalar_z.at[step], sc_send.at[step], sc_recv.at[step], near_peer).wait_recv()
        inner_sum = inner_sum + scalar_z[step]
    scalar_s[0] = inner_sum
    for step in range(1, sectors):
        at = far_count + step
        send(scalar_s.at[0], scalar_s.at[step], sc_send.at[at], sc_recv.at[at], sec_peer(step))

    direct = finish(dir_keep, dir_zr, dir_send, dir_recv)
    for step in range(1, sectors):
        at = far_count + step
        remote(scalar_s.at[step], scalar_s.at[step], sc_send.at[at], sc_recv.at[at], near_peer).wait_recv()
        inner_sum = inner_sum + scalar_s[step]
    energy_ref[...] = jnp.sum(inner_sum[0], keepdims=True) / jnp.sum(inner_sum[1], keepdims=True)

    source = jnp.int32(0)
    for sector in range(sectors):
        source = jnp.where(partner_ref[sector] == me_sec, sector, source)
    for step in range(1, sectors):
        block = routed.at[sec_at(-step)]
        remote(block, block, route_send.at[step], route_recv.at[step], near_peer).wait_recv()
    sigma_ref[0] = jnp.where(live_mask, direct + routed[source] + diag * wave, 0.0)

    for copy in started:
        copy.wait_send()


def per_device(sectors, ops, wavefunction, left_ops, right_ops, diagonal, sector_sizes, partner):
    _, rows, width = wavefunction.shape
    terms, height = left_ops.shape[1:3]
    far_count = ops // PAIR
    block16 = pltpu.VMEM((far_count, rows, width), BF16)
    block32 = pltpu.VMEM((far_count, rows, width), F32)
    gathered = pltpu.VMEM((ops, rows, width), BF16)
    full = pltpu.VMEM((height, width), BF16)
    operators = pltpu.VMEM((terms, height, width), BF16)
    dma = pltpu.SemaphoreType.DMA
    vmem = pl.BlockSpec(memory_space=pltpu.VMEM)
    smem = pl.BlockSpec(memory_space=pltpu.SMEM)
    hbm = pl.BlockSpec(memory_space=pl.ANY)
    sigma, energy = pl.pallas_call(
        functools.partial(kernel, sectors, ops),
        out_shape=(
            jax.ShapeDtypeStruct((1, rows, width), F32),
            jax.ShapeDtypeStruct((1, 1), F32),
        ),
        in_specs=[smem, smem, vmem, vmem, hbm, hbm],
        out_specs=(vmem, vmem),
        scratch_shapes=[
            operators, operators, operators, gathered, gathered, full, full,
            pltpu.VMEM((sectors, rows, width), BF16),
            pltpu.VMEM((height, width), F32),
            block32, block16, block16, block16, block16,
            pltpu.VMEM((sectors, rows, width), F32),
            block32, block16, block16, block16, block16,
            pltpu.VMEM((2, 8, 128), F32),
            pltpu.VMEM((2, 8, 128), F32),
            pltpu.VMEM((far_count, 2, 8, 128), F32),
            pltpu.VMEM((sectors, 2, 8, 128), F32),
            dma((2,)),
            *[dma((2 * far_count,))] * 4,
            *[dma((sectors,))] * 4,
            *[dma((2 * far_count,))] * 4,
            *[dma((far_count + sectors,))] * 2,
        ],
        compiler_params=pltpu.CompilerParams(
            collective_id=0, has_side_effects=True, vmem_limit_bytes=56 * 1024 * 1024
        ),
        cost_estimate=pl.CostEstimate(
            flops=8 * terms * height * height * width,
            bytes_accessed=4 * terms * height * width,
            transcendentals=0,
        ),
    )(partner, sector_sizes, wavefunction, diagonal, left_ops, right_ops)

    energy = energy[0, 0]
    row_index = lax.axis_index("op") * rows + jnp.arange(rows, dtype=jnp.int32)
    col_index = jnp.arange(width, dtype=jnp.int32)
    live_mask = (row_index[None, :, None] < sector_sizes[:, None, None]) & (
        col_index[None, None, :] < sector_sizes[:, None, None]
    )
    wave = jnp.where(live_mask, wavefunction, jnp.zeros_like(wavefunction)).astype(F32)
    residual = sigma - energy * wave
    updated = wave - residual / jnp.maximum(jnp.abs(diagonal - energy), 1.0)
    return (updated, residual)


def solution(mesh):
    return jax.shard_map(
        functools.partial(per_device, mesh.shape["sec"], mesh.shape["op"]),
        mesh=mesh,
        in_specs=(
            P("sec", "op", None),
            P("sec", "op", None, None),
            P("sec", "op", None, None),
            P("sec", "op", None),
            P("sec"),
            P(),
        ),
        out_specs=(P("sec", "op", None), P("sec", "op", None)),
        check_vma=False,
    )
```

```python
import functools

import jax
import jax.numpy as jnp
from jax import lax
from jax.experimental import pallas as pl
from jax.experimental.pallas import tpu as pltpu
from jax.sharding import PartitionSpec as P

MESH = pl.DeviceIdType.MESH
F32 = jnp.float32
BF16 = jnp.bfloat16
PAIR = 2


def nt_dot(a, b):
    return lax.dot_general(a, b, (((1,), (1,)), ((), ())), preferred_element_type=F32)


def nn_dot(a, b):
    return lax.dot_general(a, b, (((1,), (0,)), ((), ())), preferred_element_type=F32)


def fold_sum(value):
    rows, width = value.shape
    part = jnp.sum(value.reshape(rows // 8, 8, width), axis=0)
    total = part[:, :128]
    for start in range(128, width, 128):
        total = total + part[:, start : start + 128]
    return total


def kernel(
    sectors, ops,
    partner_ref, sizes_ref, wave_ref, diag_ref, left_hbm, right_hbm,
    sigma_ref, energy_ref,
    left, right, left_t, blocks, own_full, other_full, acc,
    adj_keep, adj_ys, adj_yr, adj_zs, adj_zr, routed,
    dir_keep, dir_ys, dir_yr, dir_zs, dir_zr,
    scalars, scalar_y, scalar_z, scalar_s,
    load_sem,
    chain_send, chain_recv, near_send, near_recv,
    sec_send, sec_recv, mate_send, mate_recv, route_send, route_recv,
    adj_send, adj_recv, dir_send, dir_recv, sc_send, sc_recv,
):
    far_count = ops // PAIR
    sec_far = sectors // PAIR
    me_sec = lax.axis_index("sec")
    me_op = lax.axis_index("op")
    far, near = me_op // PAIR, lax.rem(me_op, PAIR)
    chip, core = me_sec // PAIR, lax.rem(me_sec, PAIR)
    rows, width = wave_ref.shape[1:]
    terms = left.shape[0]

    def far_at(step):
        return lax.rem(far + step + far_count, far_count)

    def sec_at(step):
        return lax.rem(me_sec + step + sectors, sectors)

    def chip_at(step):
        return lax.rem(chip + step + sec_far, sec_far) * PAIR

    near_peer = (me_sec, far * PAIR + (1 - near))
    up_peer = (me_sec, me_op + PAIR)
    down_peer = (me_sec, me_op - PAIR)
    mate = (chip * PAIR + (1 - core), me_op)

    def far_peer(step):
        return (me_sec, far_at(step) * PAIR + near)

    def sec_peer(step):
        return (sec_at(step), me_op)

    def chip_peer(step):
        return (chip_at(step) + core, me_op)

    def remote(src, dst, send, recv, device):
        return pltpu.make_async_remote_copy(
            src_ref=src, dst_ref=dst, send_sem=send, recv_sem=recv, device_id=device, device_id_type=MESH
        )

    started = []

    def send(*args):
        remote(*args).start()
        started.append((None, args))

    def send_if(cond, *args):
        @pl.when(cond)
        def _():
            remote(*args).start()

        started.append((cond, args))

    def recv(dst, send_sem, recv_sem):
        remote(dst, dst, send_sem, recv_sem, near_peer).wait_recv()

    load_left = pltpu.make_async_copy(left_hbm.at[0], left, load_sem.at[0])
    load_right = pltpu.make_async_copy(right_hbm.at[0], right, load_sem.at[1])
    load_left.start()
    load_right.start()

    barrier = pltpu.get_barrier_semaphore()
    peers = [near_peer]
    peers += [far_peer(step) for step in range(1, far_count)]
    peers += [sec_peer(step) for step in range(1, sectors)]
    for peer in peers:
        pl.semaphore_signal(barrier, inc=1, device_id=peer, device_id_type=MESH)

    size = sizes_ref[0]
    row_index = me_op * rows + lax.broadcasted_iota(jnp.int32, (rows, width), 0)
    col_index = lax.broadcasted_iota(jnp.int32, (rows, width), 1)
    live_mask = (row_index < size) & (col_index < size)
    wave = jnp.where(live_mask, wave_ref[0].astype(F32), 0.0)
    blocks[me_sec, near, far] = wave.astype(BF16)
    diag = diag_ref[0]
    scalars[0] = fold_sum(diag * wave * wave)
    scalars[1] = fold_sum(wave * wave)
    pl.semaphore_wait(barrier, len(peers))

    has_up, has_down = far + 1 < far_count, far > 0

    def to_chips(cond, half, place):
        block = blocks.at[me_sec, half, place]
        for step in range(1, sec_far):
            args = (block, block, sec_send.at[step, half, place], sec_recv.at[step, half], chip_peer(step))
            send(*args) if cond is None else send_if(cond, *args)

    mine = blocks.at[me_sec, near, far]
    send_if(has_up, mine, mine, chain_send.at[0, far], chain_recv.at[far], up_peer)
    send_if(has_down, mine, mine, chain_send.at[1, far], chain_recv.at[far], down_peer)
    send(mine, mine, near_send.at[far], near_recv.at[far], near_peer)
    to_chips(None, near, far)

    def arrive(cond, place, onward, way, peer):
        block = blocks.at[me_sec, near, place]

        @pl.when(cond)
        def _():
            recv(block, chain_send.at[way, place], chain_recv.at[place])

        send_if(cond & onward, block, block, chain_send.at[way, place], chain_recv.at[place], peer)
        send_if(cond, block, block, near_send.at[place], near_recv.at[place], near_peer)
        to_chips(cond, near, place)

    load_left.wait()

    def turn(term, carry):
        left_t[term] = left[term].T
        return carry

    turned = 0
    for step in range(1, far_count):
        if turned < terms:
            turn(turned, 0)
            turned += 1
        arrive(far - step >= 0, jnp.maximum(far - step, 0), has_up, 0, up_peer)
        arrive(far + step < far_count, jnp.minimum(far + step, far_count - 1), has_down, 1, down_peer)
    for term in range(turned, terms):
        turn(term, 0)

    def to_mate(sector, step, half):
        part = blocks.at[sector, half]
        send(part, part, mate_send.at[step, half], mate_recv.at[step, half], mate)

    to_mate(me_sec, 0, near)
    for step in range(far_count):
        place = far_at(-step)
        recv(blocks.at[me_sec, 1 - near, place], near_send.at[place], near_recv.at[place])
        to_chips(None, 1 - near, place)
    to_mate(me_sec, 0, 1 - near)

    def assemble(sector, full):
        for place in range(far_count):
            pair = [blocks[sector, half, place] for half in range(PAIR)]
            if rows % 16:
                pair = [part.astype(F32) for part in pair]
            full[place * span : (place + 1) * span, :] = jnp.concatenate(pair, axis=0).astype(BF16)

    span = PAIR * rows
    assemble(me_sec, own_full)
    load_right.wait()

    order = list(range(1, far_count)) + [0]
    half = (far_count + 1) // 2
    groups = [order[:half], order[half:]]

    def place_of(step):
        return pl.ds(pl.multiple_of(far_at(step) * span, span), span)

    def products(group, base, left_side, middle, last_dot, keep, ys, yr, sends, recvs):
        total = acc.at[pl.ds(base, len(group) * span)]

        def one(term, carry):
            lhs = jnp.concatenate([left_side[term, place_of(step), :] for step in group], axis=0)
            inner = nn_dot(lhs, middle[...]).astype(BF16)
            out = last_dot(inner, right[term])

            @pl.when(term == 0)
            def _():
                total[...] = out

            @pl.when(term > 0)
            def _():
                total[...] += out

            return carry

        lax.fori_loop(0, terms, one, 0)
        for at, step in enumerate(group):
            start = base + at * span
            first = acc[start : start + rows, :]
            second = acc[start + rows : start + span, :]
            keep[step] = jnp.where(near == 0, first, second)
            ys[step] = jnp.where(near == 0, second, first).astype(BF16)
            send(ys.at[step], yr.at[step], sends.at[step], recvs.at[step], near_peer)

    def inner_product(group, base, weight):
        for at, step in enumerate(group):
            start = base + at * span
            scalars[0] += fold_sum(acc[start : start + span, :] * weight[place_of(step), :].astype(F32))

    def pass_on(step, keep, yr, zs, zr, sends, recvs):
        recv(yr.at[step], sends.at[step], recvs.at[step])
        summed = keep[step] + yr[step].astype(F32)
        if step == 0:
            keep[0] = summed
        else:
            zs[step] = summed.astype(BF16)
            at = far_count + step
            send(zs.at[step], zr.at[step], sends.at[at], recvs.at[at], far_peer(step))

    def finish(keep, zr, sends, recvs):
        total = keep[0]
        for step in range(1, far_count):
            at = far_count + step
            recv(zr.at[step], sends.at[at], recvs.at[at])
            total = total + zr[step].astype(F32)
        return total

    def from_chips(half):
        for step in range(1, sec_far):
            sector = chip_at(-step) + core
            recv(blocks.at[sector, half], sec_send.at[step, half, 0], sec_recv.at[step, half])
            to_mate(sector, step, half)

    adj = (adj_keep, adj_ys, adj_yr, adj_send, adj_recv)
    direct = (dir_keep, dir_ys, dir_yr, dir_send, dir_recv)
    adj_pass = (adj_keep, adj_yr, adj_zs, adj_zr, adj_send, adj_recv)
    dir_pass = (dir_keep, dir_yr, dir_zs, dir_zr, dir_send, dir_recv)
    second_base = len(groups[0]) * span

    products(groups[0], 0, left_t, own_full, nn_dot, *adj)
    from_chips(near)
    products(groups[1], second_base, left_t, own_full, nn_dot, *adj)
    for step in groups[0]:
        pass_on(step, *adj_pass)
    from_chips(1 - near)
    for step in range(sec_far):
        sector = chip_at(-step) + (1 - core)
        for side in (near, 1 - near):
            recv(blocks.at[sector, side], mate_send.at[step, side], mate_recv.at[step, side])
    assemble(partner_ref[me_sec], other_full)
    inner_product(groups[0], 0, other_full)
    inner_product(groups[1], second_base, other_full)

    products(groups[0], 0, left, other_full, nt_dot, *direct)
    for step in groups[1]:
        pass_on(step, *adj_pass)
    products(groups[1], second_base, left, other_full, nt_dot, *direct)
    for step in groups[0]:
        pass_on(step, *dir_pass)
    inner_product(groups[0], 0, own_full)
    inner_product(groups[1], second_base, own_full)

    send(scalars, scalar_y, sc_send.at[0], sc_recv.at[0], near_peer)
    routed[me_sec] = finish(adj_keep, adj_zr, adj_send, adj_recv)
    rows_out = routed.at[me_sec]
    for step in range(1, sec_far):
        send(rows_out, rows_out, route_send.at[0, step], route_recv.at[0, step], chip_peer(step))
    send(rows_out, rows_out, route_send.at[1, 0], route_recv.at[1, 0], mate)
    recv(scalar_y, sc_send.at[0], sc_recv.at[0])
    scalar_z[0] = scalars[...] + scalar_y[...]
    for step in range(1, far_count):
        send(scalar_z.at[0], scalar_z.at[step], sc_send.at[step], sc_recv.at[step], far_peer(step))
    for step in groups[1]:
        pass_on(step, *dir_pass)

    inner_sum = scalar_z[0]
    for step in range(1, far_count):
        recv(scalar_z.at[step], sc_send.at[step], sc_recv.at[step])
        inner_sum = inner_sum + scalar_z[step]
    scalar_s[0] = inner_sum
    for step in range(1, sectors):
        at = far_count + step
        send(scalar_s.at[0], scalar_s.at[step], sc_send.at[at], sc_recv.at[at], sec_peer(step))
    for step in range(1, sec_far):
        part = routed.at[chip_at(-step) + core]
        recv(part, route_send.at[0, step], route_recv.at[0, step])
        send(part, part, route_send.at[1, step], route_recv.at[1, step], mate)
    for step in range(1, sectors):
        at = far_count + step
        recv(scalar_s.at[step], sc_send.at[at], sc_recv.at[at])
        inner_sum = inner_sum + scalar_s[step]
    energy_ref[...] = jnp.sum(inner_sum[0], keepdims=True) / jnp.sum(inner_sum[1], keepdims=True)

    source = jnp.int32(0)
    for sector in range(sectors):
        source = jnp.where(partner_ref[sector] == me_sec, sector, source)
    for step in range(sec_far):
        recv(routed.at[chip_at(-step) + (1 - core)], route_send.at[1, step], route_recv.at[1, step])
    other_part = routed[source] + diag_ref[0] * wave
    direct_part = finish(dir_keep, dir_zr, dir_send, dir_recv)
    sigma_ref[0] = jnp.where(live_mask, direct_part + other_part, 0.0)

    for cond, args in started:
        if cond is None:
            remote(*args).wait_send()
        else:

            @pl.when(cond)
            def _():
                remote(*args).wait_send()


def per_device(sectors, ops, wavefunction, left_ops, right_ops, diagonal, sector_sizes, partner):
    _, rows, width = wavefunction.shape
    terms, height = left_ops.shape[1:3]
    far_count = ops // PAIR
    block16 = pltpu.VMEM((far_count, rows, width), BF16)
    block32 = pltpu.VMEM((far_count, rows, width), F32)
    sec_far = sectors // PAIR
    full = pltpu.VMEM((height, width), BF16)
    operators = pltpu.VMEM((terms, height, width), BF16)
    dma = pltpu.SemaphoreType.DMA
    vmem = pl.BlockSpec(memory_space=pltpu.VMEM)
    smem = pl.BlockSpec(memory_space=pltpu.SMEM)
    hbm = pl.BlockSpec(memory_space=pl.ANY)
    sigma, energy = pl.pallas_call(
        functools.partial(kernel, sectors, ops),
        out_shape=(
            jax.ShapeDtypeStruct((1, rows, width), F32),
            jax.ShapeDtypeStruct((1, 1), F32),
        ),
        in_specs=[smem, smem, vmem, vmem, hbm, hbm],
        out_specs=(vmem, vmem),
        scratch_shapes=[
            operators, operators, operators,
            pltpu.VMEM((sectors, PAIR, far_count, rows, width), BF16),
            full, full,
            pltpu.VMEM((height, width), F32),
            block32, block16, block16, block16, block16,
            pltpu.VMEM((sectors, rows, width), F32),
            block32, block16, block16, block16, block16,
            pltpu.VMEM((2, 8, 128), F32),
            pltpu.VMEM((2, 8, 128), F32),
            pltpu.VMEM((far_count, 2, 8, 128), F32),
            pltpu.VMEM((sectors, 2, 8, 128), F32),
            dma((2,)),
            dma((2, far_count)), *[dma((far_count,))] * 3,
            dma((sec_far, PAIR, far_count)), dma((sec_far, PAIR)),
            *[dma((sec_far, PAIR))] * 2,
            *[dma((2, sec_far))] * 2,
            *[dma((2 * far_count,))] * 4,
            *[dma((far_count + sectors,))] * 2,
        ],
        compiler_params=pltpu.CompilerParams(
            collective_id=0, has_side_effects=True, vmem_limit_bytes=56 * 1024 * 1024
        ),
        cost_estimate=pl.CostEstimate(
            flops=8 * terms * height * height * width,
            bytes_accessed=4 * terms * height * width,
            transcendentals=0,
        ),
    )(partner, sector_sizes, wavefunction, diagonal, left_ops, right_ops)

    energy = energy[0, 0]
    row_index = lax.axis_index("op") * rows + jnp.arange(rows, dtype=jnp.int32)
    col_index = jnp.arange(width, dtype=jnp.int32)
    live_mask = (row_index[None, :, None] < sector_sizes[:, None, None]) & (
        col_index[None, None, :] < sector_sizes[:, None, None]
    )
    wave = jnp.where(live_mask, wavefunction, jnp.zeros_like(wavefunction)).astype(F32)
    residual = sigma - energy * wave
    updated = wave - residual / jnp.maximum(jnp.abs(diagonal - energy), 1.0)
    return (updated, residual)


def solution(mesh):
    return jax.shard_map(
        functools.partial(per_device, mesh.shape["sec"], mesh.shape["op"]),
        mesh=mesh,
        in_specs=(
            P("sec", "op", None),
            P("sec", "op", None, None),
            P("sec", "op", None, None),
            P("sec", "op", None),
            P("sec"),
            P(),
        ),
        out_specs=(P("sec", "op", None), P("sec", "op", None)),
        check_vma=False,
    )
```

```python
import functools

import jax
import jax.numpy as jnp
from jax import lax
from jax.experimental import pallas as pl
from jax.experimental.pallas import tpu as pltpu
from jax.sharding import PartitionSpec as P

MESH = pl.DeviceIdType.MESH
F32 = jnp.float32
BF16 = jnp.bfloat16
PAIR = 2


def nt_dot(a, b):
    return lax.dot_general(a, b, (((1,), (1,)), ((), ())), preferred_element_type=F32)


def nn_dot(a, b):
    return lax.dot_general(a, b, (((1,), (0,)), ((), ())), preferred_element_type=F32)


def fold_sum(value):
    rows, width = value.shape
    part = jnp.sum(value.reshape(rows // 8, 8, width), axis=0)
    total = part[:, :128]
    for start in range(128, width, 128):
        total = total + part[:, start : start + 128]
    return total


def kernel(
    sectors, ops,
    partner_ref, sizes_ref, wave_ref, diag_ref, left_hbm, right_hbm,
    sigma_ref, energy_ref,
    left, right, left_t, blocks, own_full, other_full, acc,
    adj_keep, adj_ys, adj_yr, adj_zs, adj_zr, routed,
    dir_keep, dir_ys, dir_yr, dir_zs, dir_zr,
    scalars, scalar_y, scalar_z, scalar_s,
    load_sem,
    chain_send, chain_recv, near_send, near_recv,
    sec_send, sec_recv, swap_send, swap_recv, mate_send, mate_recv, route_send, route_recv,
    adj_send, adj_recv, dir_send, dir_recv, sc_send, sc_recv,
):
    far_count = ops // PAIR
    sec_far = sectors // PAIR
    me_sec = lax.axis_index("sec")
    me_op = lax.axis_index("op")
    far, near = me_op // PAIR, lax.rem(me_op, PAIR)
    chip, core = me_sec // PAIR, lax.rem(me_sec, PAIR)
    rows, width = wave_ref.shape[1:]
    terms = left.shape[0]

    def far_at(step):
        return lax.rem(far + step + far_count, far_count)

    def sec_at(step):
        return lax.rem(me_sec + step + sectors, sectors)

    def chip_at(step):
        return lax.rem(chip + step + sec_far, sec_far) * PAIR

    near_peer = (me_sec, far * PAIR + (1 - near))
    up_peer = (me_sec, me_op + PAIR)
    down_peer = (me_sec, me_op - PAIR)
    mate = (chip * PAIR + (1 - core), me_op)

    def far_peer(step):
        return (me_sec, far_at(step) * PAIR + near)

    def sec_peer(step):
        return (sec_at(step), me_op)

    def chip_peer(step):
        return (chip_at(step) + core, me_op)

    def remote(src, dst, send, recv, device):
        return pltpu.make_async_remote_copy(
            src_ref=src, dst_ref=dst, send_sem=send, recv_sem=recv, device_id=device, device_id_type=MESH
        )

    started = []

    def send(*args):
        remote(*args).start()
        started.append((None, args))

    def send_if(cond, *args):
        @pl.when(cond)
        def _():
            remote(*args).start()

        started.append((cond, args))

    def recv(dst, send_sem, recv_sem):
        remote(dst, dst, send_sem, recv_sem, near_peer).wait_recv()

    load_left = pltpu.make_async_copy(left_hbm.at[0], left, load_sem.at[0])
    load_right = pltpu.make_async_copy(right_hbm.at[0], right, load_sem.at[1])
    load_left.start()
    load_right.start()

    barrier = pltpu.get_barrier_semaphore()
    peers = [near_peer]
    peers += [far_peer(step) for step in range(1, far_count)]
    peers += [sec_peer(step) for step in range(1, sectors)]
    for peer in peers:
        pl.semaphore_signal(barrier, inc=1, device_id=peer, device_id_type=MESH)

    size = sizes_ref[0]
    row_index = me_op * rows + lax.broadcasted_iota(jnp.int32, (rows, width), 0)
    col_index = lax.broadcasted_iota(jnp.int32, (rows, width), 1)
    live_mask = (row_index < size) & (col_index < size)
    wave = jnp.where(live_mask, wave_ref[0].astype(F32), 0.0)
    blocks[me_sec, near, far] = wave.astype(BF16)
    diag = diag_ref[0]
    scalars[0] = fold_sum(diag * wave * wave)
    scalars[1] = fold_sum(wave * wave)
    pl.semaphore_wait(barrier, len(peers))

    has_up, has_down = far + 1 < far_count, far > 0

    def to_chips(cond, half, place):
        block = blocks.at[me_sec, half, place]
        for step in range(1, sec_far):
            args = (block, block, sec_send.at[step, half, place], sec_recv.at[step, half, place], chip_peer(step))
            send(*args) if cond is None else send_if(cond, *args)

    mine = blocks.at[me_sec, near, far]
    send_if(has_up, mine, mine, chain_send.at[0, far], chain_recv.at[far], up_peer)
    send_if(has_down, mine, mine, chain_send.at[1, far], chain_recv.at[far], down_peer)
    send(mine, mine, near_send.at[far], near_recv.at[far], near_peer)
    to_chips(None, near, far)

    def arrive(cond, place, onward, way, peer):
        block = blocks.at[me_sec, near, place]

        @pl.when(cond)
        def _():
            recv(block, chain_send.at[way, place], chain_recv.at[place])

        send_if(cond & onward, block, block, chain_send.at[way, place], chain_recv.at[place], peer)
        send_if(cond, block, block, near_send.at[place], near_recv.at[place], near_peer)
        to_chips(cond, near, place)

    load_left.wait()

    def turn(term, carry):
        left_t[term] = left[term].T
        return carry

    turned = 0
    for step in range(1, far_count):
        if turned < terms:
            turn(turned, 0)
            turned += 1
        arrive(far - step >= 0, jnp.maximum(far - step, 0), has_up, 0, up_peer)
        arrive(far + step < far_count, jnp.minimum(far + step, far_count - 1), has_down, 1, down_peer)
    for term in range(turned, terms):
        turn(term, 0)

    def to_mate(sector, step, half):
        part = blocks.at[sector, half]
        send(part, part, mate_send.at[step, half], mate_recv.at[step, half], mate)

    beside = far + 1 - 2 * lax.rem(far, PAIR)
    rest = []
    for step in range(1, far_count // PAIR):
        base = lax.rem(far // PAIR + step, far_count // PAIR) * PAIR
        rest += [base, base + 1]
    for place in (far, beside):
        for step in range(1, sec_far):
            block = blocks.at[chip_at(-step) + core, near, place]
            recv(block, sec_send.at[step, near, place], sec_recv.at[step, near, place])
            send(block, block, swap_send.at[step, place], swap_recv.at[step, place], near_peer)

    to_mate(me_sec, 0, near)
    for place in (far, beside):
        recv(blocks.at[me_sec, 1 - near, place], near_send.at[place], near_recv.at[place])
    for place in rest:
        recv(blocks.at[me_sec, 1 - near, place], near_send.at[place], near_recv.at[place])
        to_chips(None, 1 - near, place)
    to_mate(me_sec, 0, 1 - near)

    def assemble(sector, full):
        for place in range(far_count):
            pair = [blocks[sector, half, place] for half in range(PAIR)]
            if rows % 16:
                pair = [part.astype(F32) for part in pair]
            full[place * span : (place + 1) * span, :] = jnp.concatenate(pair, axis=0).astype(BF16)

    span = PAIR * rows
    assemble(me_sec, own_full)
    load_right.wait()

    order = list(range(1, far_count)) + [0]
    half = (far_count + 1) // 2
    groups = [order[:half], order[half:]]

    def place_of(step):
        return pl.ds(pl.multiple_of(far_at(step) * span, span), span)

    def products(group, base, left_side, middle, last_dot, keep, ys, yr, sends, recvs):
        total = acc.at[pl.ds(base, len(group) * span)]

        def one(term, carry):
            lhs = jnp.concatenate([left_side[term, place_of(step), :] for step in group], axis=0)
            inner = nn_dot(lhs, middle[...]).astype(BF16)
            out = last_dot(inner, right[term])

            @pl.when(term == 0)
            def _():
                total[...] = out

            @pl.when(term > 0)
            def _():
                total[...] += out

            return carry

        lax.fori_loop(0, terms, one, 0)
        for at, step in enumerate(group):
            start = base + at * span
            first = acc[start : start + rows, :]
            second = acc[start + rows : start + span, :]
            keep[step] = jnp.where(near == 0, first, second)
            ys[step] = jnp.where(near == 0, second, first).astype(BF16)
            send(ys.at[step], yr.at[step], sends.at[step], recvs.at[step], near_peer)

    def inner_product(group, base, weight):
        for at, step in enumerate(group):
            start = base + at * span
            scalars[0] += fold_sum(acc[start : start + span, :] * weight[place_of(step), :].astype(F32))

    def pass_on(step, keep, yr, zs, zr, sends, recvs):
        recv(yr.at[step], sends.at[step], recvs.at[step])
        summed = keep[step] + yr[step].astype(F32)
        if step == 0:
            keep[0] = summed
        else:
            zs[step] = summed.astype(BF16)
            at = far_count + step
            send(zs.at[step], zr.at[step], sends.at[at], recvs.at[at], far_peer(step))

    def finish(keep, zr, sends, recvs):
        total = keep[0]
        for step in range(1, far_count):
            at = far_count + step
            recv(zr.at[step], sends.at[at], recvs.at[at])
            total = total + zr[step].astype(F32)
        return total

    def from_chips(half, direct_half):
        for step in range(1, sec_far):
            sector = chip_at(-step) + core
            if not direct_half:
                for place in (far, beside):
                    recv(blocks.at[sector, half, place], swap_send.at[step, place], swap_recv.at[step, place])
            for place in rest:
                recv(blocks.at[sector, half, place], sec_send.at[step, half, place], sec_recv.at[step, half, place])
            to_mate(sector, step, half)

    adj = (adj_keep, adj_ys, adj_yr, adj_send, adj_recv)
    direct = (dir_keep, dir_ys, dir_yr, dir_send, dir_recv)
    adj_pass = (adj_keep, adj_yr, adj_zs, adj_zr, adj_send, adj_recv)
    dir_pass = (dir_keep, dir_yr, dir_zs, dir_zr, dir_send, dir_recv)
    second_base = len(groups[0]) * span

    products(groups[0], 0, left_t, own_full, nn_dot, *adj)
    from_chips(near, True)
    products(groups[1], second_base, left_t, own_full, nn_dot, *adj)
    for step in groups[0]:
        pass_on(step, *adj_pass)
    from_chips(1 - near, False)
    for step in range(sec_far):
        sector = chip_at(-step) + (1 - core)
        for side in (near, 1 - near):
            recv(blocks.at[sector, side], mate_send.at[step, side], mate_recv.at[step, side])
    assemble(partner_ref[me_sec], other_full)
    inner_product(groups[0], 0, other_full)
    inner_product(groups[1], second_base, other_full)

    products(groups[0], 0, left, other_full, nt_dot, *direct)
    for step in groups[1]:
        pass_on(step, *adj_pass)
    products(groups[1], second_base, left, other_full, nt_dot, *direct)
    for step in groups[0]:
        pass_on(step, *dir_pass)
    inner_product(groups[0], 0, own_full)
    inner_product(groups[1], second_base, own_full)

    send(scalars, scalar_y, sc_send.at[0], sc_recv.at[0], near_peer)
    routed[me_sec] = finish(adj_keep, adj_zr, adj_send, adj_recv)
    rows_out = routed.at[me_sec]
    for step in range(1, sec_far):
        send(rows_out, rows_out, route_send.at[0, step], route_recv.at[0, step], chip_peer(step))
    send(rows_out, rows_out, route_send.at[1, 0], route_recv.at[1, 0], mate)
    recv(scalar_y, sc_send.at[0], sc_recv.at[0])
    scalar_z[0] = scalars[...] + scalar_y[...]
    for step in range(1, far_count):
        send(scalar_z.at[0], scalar_z.at[step], sc_send.at[step], sc_recv.at[step], far_peer(step))
    for step in groups[1]:
        pass_on(step, *dir_pass)

    inner_sum = scalar_z[0]
    for step in range(1, far_count):
        recv(scalar_z.at[step], sc_send.at[step], sc_recv.at[step])
        inner_sum = inner_sum + scalar_z[step]
    scalar_s[0] = inner_sum
    for step in range(1, sectors):
        at = far_count + step
        send(scalar_s.at[0], scalar_s.at[step], sc_send.at[at], sc_recv.at[at], sec_peer(step))
    for step in range(1, sec_far):
        part = routed.at[chip_at(-step) + core]
        recv(part, route_send.at[0, step], route_recv.at[0, step])
        send(part, part, route_send.at[1, step], route_recv.at[1, step], mate)
    for step in range(1, sectors):
        at = far_count + step
        recv(scalar_s.at[step], sc_send.at[at], sc_recv.at[at])
        inner_sum = inner_sum + scalar_s[step]
    energy_ref[...] = jnp.sum(inner_sum[0], keepdims=True) / jnp.sum(inner_sum[1], keepdims=True)

    source = jnp.int32(0)
    for sector in range(sectors):
        source = jnp.where(partner_ref[sector] == me_sec, sector, source)
    for step in range(sec_far):
        recv(routed.at[chip_at(-step) + (1 - core)], route_send.at[1, step], route_recv.at[1, step])
    other_part = routed[source] + diag_ref[0] * wave
    direct_part = finish(dir_keep, dir_zr, dir_send, dir_recv)
    sigma_ref[0] = jnp.where(live_mask, direct_part + other_part, 0.0)

    for cond, args in started:
        if cond is None:
            remote(*args).wait_send()
        else:

            @pl.when(cond)
            def _():
                remote(*args).wait_send()


def per_device(sectors, ops, wavefunction, left_ops, right_ops, diagonal, sector_sizes, partner):
    _, rows, width = wavefunction.shape
    terms, height = left_ops.shape[1:3]
    far_count = ops // PAIR
    block16 = pltpu.VMEM((far_count, rows, width), BF16)
    block32 = pltpu.VMEM((far_count, rows, width), F32)
    sec_far = sectors // PAIR
    full = pltpu.VMEM((height, width), BF16)
    operators = pltpu.VMEM((terms, height, width), BF16)
    dma = pltpu.SemaphoreType.DMA
    vmem = pl.BlockSpec(memory_space=pltpu.VMEM)
    smem = pl.BlockSpec(memory_space=pltpu.SMEM)
    hbm = pl.BlockSpec(memory_space=pl.ANY)
    sigma, energy = pl.pallas_call(
        functools.partial(kernel, sectors, ops),
        out_shape=(
            jax.ShapeDtypeStruct((1, rows, width), F32),
            jax.ShapeDtypeStruct((1, 1), F32),
        ),
        in_specs=[smem, smem, vmem, vmem, hbm, hbm],
        out_specs=(vmem, vmem),
        scratch_shapes=[
            operators, operators, operators,
            pltpu.VMEM((sectors, PAIR, far_count, rows, width), BF16),
            full, full,
            pltpu.VMEM((height, width), F32),
            block32, block16, block16, block16, block16,
            pltpu.VMEM((sectors, rows, width), F32),
            block32, block16, block16, block16, block16,
            pltpu.VMEM((2, 8, 128), F32),
            pltpu.VMEM((2, 8, 128), F32),
            pltpu.VMEM((far_count, 2, 8, 128), F32),
            pltpu.VMEM((sectors, 2, 8, 128), F32),
            dma((2,)),
            dma((2, far_count)), *[dma((far_count,))] * 3,
            *[dma((sec_far, PAIR, far_count))] * 2,
            *[dma((sec_far, far_count))] * 2,
            *[dma((sec_far, PAIR))] * 2,
            *[dma((2, sec_far))] * 2,
            *[dma((2 * far_count,))] * 4,
            *[dma((far_count + sectors,))] * 2,
        ],
        compiler_params=pltpu.CompilerParams(
            collective_id=0, has_side_effects=True, vmem_limit_bytes=56 * 1024 * 1024
        ),
        cost_estimate=pl.CostEstimate(
            flops=8 * terms * height * height * width,
            bytes_accessed=4 * terms * height * width,
            transcendentals=0,
        ),
    )(partner, sector_sizes, wavefunction, diagonal, left_ops, right_ops)

    energy = energy[0, 0]
    row_index = lax.axis_index("op") * rows + jnp.arange(rows, dtype=jnp.int32)
    col_index = jnp.arange(width, dtype=jnp.int32)
    live_mask = (row_index[None, :, None] < sector_sizes[:, None, None]) & (
        col_index[None, None, :] < sector_sizes[:, None, None]
    )
    wave = jnp.where(live_mask, wavefunction, jnp.zeros_like(wavefunction)).astype(F32)
    residual = sigma - energy * wave
    updated = wave - residual / jnp.maximum(jnp.abs(diagonal - energy), 1.0)
    return (updated, residual)


def solution(mesh):
    return jax.shard_map(
        functools.partial(per_device, mesh.shape["sec"], mesh.shape["op"]),
        mesh=mesh,
        in_specs=(
            P("sec", "op", None),
            P("sec", "op", None, None),
            P("sec", "op", None, None),
            P("sec", "op", None),
            P("sec"),
            P(),
        ),
        out_specs=(P("sec", "op", None), P("sec", "op", None)),
        check_vma=False,
    )
```

```python
import functools

import jax
import jax.numpy as jnp
from jax import lax
from jax.experimental import pallas as pl
from jax.experimental.pallas import tpu as pltpu
from jax.sharding import PartitionSpec as P

MESH = pl.DeviceIdType.MESH
F32 = jnp.float32
BF16 = jnp.bfloat16
PAIR = 2


def nt_dot(a, b):
    return lax.dot_general(a, b, (((1,), (1,)), ((), ())), preferred_element_type=F32)


def nn_dot(a, b):
    return lax.dot_general(a, b, (((1,), (0,)), ((), ())), preferred_element_type=F32)


def fold_sum(value):
    rows, width = value.shape
    part = jnp.sum(value.reshape(rows // 8, 8, width), axis=0)
    total = part[:, :128]
    for start in range(128, width, 128):
        total = total + part[:, start : start + 128]
    return total


def kernel(
    sectors, ops,
    partner_ref, sizes_ref, wave_ref, diag_ref, left_hbm, right_hbm,
    sigma_ref, energy_ref,
    left, right, left_t, blocks, own_full, other_full, inner, acc,
    adj_keep, adj_ys, adj_yr, adj_zs, adj_zr, routed,
    dir_keep, dir_ys, dir_yr, dir_zs, dir_zr,
    scalars, scalar_y, scalar_z, scalar_s,
    load_sem,
    chain_send, chain_recv, near_send, near_recv,
    sec_send, sec_recv, mate_send, mate_recv, route_send, route_recv,
    adj_send, adj_recv, dir_send, dir_recv, sc_send, sc_recv,
):
    far_count = ops // PAIR
    sec_far = sectors // PAIR
    me_sec = lax.axis_index("sec")
    me_op = lax.axis_index("op")
    far, near = me_op // PAIR, lax.rem(me_op, PAIR)
    chip, core = me_sec // PAIR, lax.rem(me_sec, PAIR)
    rows, width = wave_ref.shape[1:]
    terms = left.shape[0]

    def far_at(step):
        return lax.rem(far + step + far_count, far_count)

    def sec_at(step):
        return lax.rem(me_sec + step + sectors, sectors)

    def chip_at(step):
        return lax.rem(chip + step + sec_far, sec_far) * PAIR

    near_peer = (me_sec, far * PAIR + (1 - near))
    up_peer = (me_sec, me_op + PAIR)
    down_peer = (me_sec, me_op - PAIR)
    mate = (chip * PAIR + (1 - core), me_op)

    def far_peer(step):
        return (me_sec, far_at(step) * PAIR + near)

    def sec_peer(step):
        return (sec_at(step), me_op)

    def chip_peer(step):
        return (chip_at(step) + core, me_op)

    def remote(src, dst, send, recv, device):
        return pltpu.make_async_remote_copy(
            src_ref=src, dst_ref=dst, send_sem=send, recv_sem=recv, device_id=device, device_id_type=MESH
        )

    started = []

    def send(*args):
        remote(*args).start()
        started.append((None, args))

    def send_if(cond, *args):
        @pl.when(cond)
        def _():
            remote(*args).start()

        started.append((cond, args))

    def recv(dst, send_sem, recv_sem):
        remote(dst, dst, send_sem, recv_sem, near_peer).wait_recv()

    load_left = pltpu.make_async_copy(left_hbm.at[0], left, load_sem.at[0])
    load_right = pltpu.make_async_copy(right_hbm.at[0], right, load_sem.at[1])
    load_left.start()
    load_right.start()

    barrier = pltpu.get_barrier_semaphore()
    peers = [near_peer]
    peers += [far_peer(step) for step in range(1, far_count)]
    peers += [sec_peer(step) for step in range(1, sectors)]
    for peer in peers:
        pl.semaphore_signal(barrier, inc=1, device_id=peer, device_id_type=MESH)

    size = sizes_ref[0]
    row_index = me_op * rows + lax.broadcasted_iota(jnp.int32, (rows, width), 0)
    col_index = lax.broadcasted_iota(jnp.int32, (rows, width), 1)
    live_mask = (row_index < size) & (col_index < size)
    wave = jnp.where(live_mask, wave_ref[0].astype(F32), 0.0)
    blocks[me_sec, near, far] = wave.astype(BF16)
    diag = diag_ref[0]
    scalars[0] = fold_sum(diag * wave * wave)
    scalars[1] = fold_sum(wave * wave)
    pl.semaphore_wait(barrier, len(peers))

    has_up, has_down = far + 1 < far_count, far > 0

    def to_chips(cond, half, place):
        block = blocks.at[me_sec, half, place]
        for step in range(1, sec_far):
            args = (block, block, sec_send.at[step, half, place], sec_recv.at[step, half], chip_peer(step))
            send(*args) if cond is None else send_if(cond, *args)

    mine = blocks.at[me_sec, near, far]
    send_if(has_up, mine, mine, chain_send.at[0, far], chain_recv.at[far], up_peer)
    send_if(has_down, mine, mine, chain_send.at[1, far], chain_recv.at[far], down_peer)
    send(mine, mine, near_send.at[far], near_recv.at[far], near_peer)
    to_chips(None, near, far)

    def arrive(cond, place, onward, way, peer):
        block = blocks.at[me_sec, near, place]

        @pl.when(cond)
        def _():
            recv(block, chain_send.at[way, place], chain_recv.at[place])

        send_if(cond & onward, block, block, chain_send.at[way, place], chain_recv.at[place], peer)
        send_if(cond, block, block, near_send.at[place], near_recv.at[place], near_peer)
        to_chips(cond, near, place)

    load_left.wait()

    def turn(term, carry):
        left_t[term] = left[term].T
        return carry

    turned = 0
    for step in range(1, far_count):
        if turned < terms:
            turn(turned, 0)
            turned += 1
        arrive(far - step >= 0, jnp.maximum(far - step, 0), has_up, 0, up_peer)
        arrive(far + step < far_count, jnp.minimum(far + step, far_count - 1), has_down, 1, down_peer)
    for term in range(turned, terms):
        turn(term, 0)

    def to_mate(sector, step, half):
        part = blocks.at[sector, half]
        send(part, part, mate_send.at[step, half], mate_recv.at[step, half], mate)

    to_mate(me_sec, 0, near)
    for step in range(far_count):
        place = far_at(-step)
        recv(blocks.at[me_sec, 1 - near, place], near_send.at[place], near_recv.at[place])
        to_chips(None, 1 - near, place)
    to_mate(me_sec, 0, 1 - near)

    def assemble(sector, full):
        for place in range(far_count):
            pair = [blocks[sector, half, place] for half in range(PAIR)]
            if rows % 16:
                pair = [part.astype(F32) for part in pair]
            full[place * span : (place + 1) * span, :] = jnp.concatenate(pair, axis=0).astype(BF16)

    span = PAIR * rows
    assemble(me_sec, own_full)
    load_right.wait()

    order = list(range(1, far_count)) + [0]
    half = (far_count + 1) // 2
    groups = [order[:half], order[half:]]

    def place_of(step):
        return pl.ds(pl.multiple_of(far_at(step) * span, span), span)

    def first_products(left_side, middle):
        def one(term, carry):
            columns = pl.ds(pl.multiple_of(term * width, width), width)
            inner[:, columns] = nn_dot(left_side[term], middle[...]).astype(BF16)
            return carry

        lax.fori_loop(0, terms, one, 0)

    def adjoint_sum(lhs):
        return nn_dot(lhs, right[...].reshape(terms * width, width))

    def direct_sum(lhs):
        total = nt_dot(lhs[:, :width], right[0])
        for term in range(1, terms):
            total = total + nt_dot(lhs[:, term * width : (term + 1) * width], right[term])
        return total

    def products(group, base, term_sum, keep, ys, yr, sends, recvs):
        lhs = jnp.concatenate([inner[place_of(step), :] for step in group], axis=0)
        acc[base : base + len(group) * span, :] = term_sum(lhs)
        for at, step in enumerate(group):
            start = base + at * span
            first = acc[start : start + rows, :]
            second = acc[start + rows : start + span, :]
            keep[step] = jnp.where(near == 0, first, second)
            ys[step] = jnp.where(near == 0, second, first).astype(BF16)
            send(ys.at[step], yr.at[step], sends.at[step], recvs.at[step], near_peer)

    def inner_product(group, base, weight):
        for at, step in enumerate(group):
            start = base + at * span
            scalars[0] += fold_sum(acc[start : start + span, :] * weight[place_of(step), :].astype(F32))

    def pass_on(step, keep, yr, zs, zr, sends, recvs):
        recv(yr.at[step], sends.at[step], recvs.at[step])
        summed = keep[step] + yr[step].astype(F32)
        if step == 0:
            keep[0] = summed
        else:
            zs[step] = summed.astype(BF16)
            at = far_count + step
            send(zs.at[step], zr.at[step], sends.at[at], recvs.at[at], far_peer(step))

    def finish(keep, zr, sends, recvs):
        total = keep[0]
        for step in range(1, far_count):
            at = far_count + step
            recv(zr.at[step], sends.at[at], recvs.at[at])
            total = total + zr[step].astype(F32)
        return total

    def from_chips(half):
        for step in range(1, sec_far):
            sector = chip_at(-step) + core
            recv(blocks.at[sector, half], sec_send.at[step, half, 0], sec_recv.at[step, half])
            to_mate(sector, step, half)

    adj = (adj_keep, adj_ys, adj_yr, adj_send, adj_recv)
    direct = (dir_keep, dir_ys, dir_yr, dir_send, dir_recv)
    adj_pass = (adj_keep, adj_yr, adj_zs, adj_zr, adj_send, adj_recv)
    dir_pass = (dir_keep, dir_yr, dir_zs, dir_zr, dir_send, dir_recv)
    second_base = len(groups[0]) * span

    first_products(left_t, own_full)
    products(groups[0], 0, adjoint_sum, *adj)
    from_chips(near)
    products(groups[1], second_base, adjoint_sum, *adj)
    for step in groups[0]:
        pass_on(step, *adj_pass)
    from_chips(1 - near)
    for step in range(sec_far):
        sector = chip_at(-step) + (1 - core)
        for side in (near, 1 - near):
            recv(blocks.at[sector, side], mate_send.at[step, side], mate_recv.at[step, side])
    assemble(partner_ref[me_sec], other_full)
    inner_product(groups[0], 0, other_full)
    inner_product(groups[1], second_base, other_full)

    first_products(left, other_full)
    products(groups[0], 0, direct_sum, *direct)
    for step in groups[1]:
        pass_on(step, *adj_pass)
    products(groups[1], second_base, direct_sum, *direct)
    for step in groups[0]:
        pass_on(step, *dir_pass)
    inner_product(groups[0], 0, own_full)
    inner_product(groups[1], second_base, own_full)

    send(scalars, scalar_y, sc_send.at[0], sc_recv.at[0], near_peer)
    routed[me_sec] = finish(adj_keep, adj_zr, adj_send, adj_recv)
    rows_out = routed.at[me_sec]
    for step in range(1, sec_far):
        send(rows_out, rows_out, route_send.at[0, step], route_recv.at[0, step], chip_peer(step))
    send(rows_out, rows_out, route_send.at[1, 0], route_recv.at[1, 0], mate)
    recv(scalar_y, sc_send.at[0], sc_recv.at[0])
    scalar_z[0] = scalars[...] + scalar_y[...]
    for step in range(1, far_count):
        send(scalar_z.at[0], scalar_z.at[step], sc_send.at[step], sc_recv.at[step], far_peer(step))
    for step in groups[1]:
        pass_on(step, *dir_pass)

    inner_sum = scalar_z[0]
    for step in range(1, far_count):
        recv(scalar_z.at[step], sc_send.at[step], sc_recv.at[step])
        inner_sum = inner_sum + scalar_z[step]
    scalar_s[0] = inner_sum
    for step in range(1, sectors):
        at = far_count + step
        send(scalar_s.at[0], scalar_s.at[step], sc_send.at[at], sc_recv.at[at], sec_peer(step))
    for step in range(1, sec_far):
        part = routed.at[chip_at(-step) + core]
        recv(part, route_send.at[0, step], route_recv.at[0, step])
        send(part, part, route_send.at[1, step], route_recv.at[1, step], mate)
    for step in range(1, sectors):
        at = far_count + step
        recv(scalar_s.at[step], sc_send.at[at], sc_recv.at[at])
        inner_sum = inner_sum + scalar_s[step]
    energy_ref[...] = jnp.sum(inner_sum[0], keepdims=True) / jnp.sum(inner_sum[1], keepdims=True)

    source = jnp.int32(0)
    for sector in range(sectors):
        source = jnp.where(partner_ref[sector] == me_sec, sector, source)
    for step in range(sec_far):
        recv(routed.at[chip_at(-step) + (1 - core)], route_send.at[1, step], route_recv.at[1, step])
    other_part = routed[source] + diag_ref[0] * wave
    direct_part = finish(dir_keep, dir_zr, dir_send, dir_recv)
    sigma_ref[0] = jnp.where(live_mask, direct_part + other_part, 0.0)

    for cond, args in started:
        if cond is None:
            remote(*args).wait_send()
        else:

            @pl.when(cond)
            def _():
                remote(*args).wait_send()


def per_device(sectors, ops, wavefunction, left_ops, right_ops, diagonal, sector_sizes, partner):
    _, rows, width = wavefunction.shape
    terms, height = left_ops.shape[1:3]
    far_count = ops // PAIR
    block16 = pltpu.VMEM((far_count, rows, width), BF16)
    block32 = pltpu.VMEM((far_count, rows, width), F32)
    sec_far = sectors // PAIR
    full = pltpu.VMEM((height, width), BF16)
    operators = pltpu.VMEM((terms, height, width), BF16)
    dma = pltpu.SemaphoreType.DMA
    vmem = pl.BlockSpec(memory_space=pltpu.VMEM)
    smem = pl.BlockSpec(memory_space=pltpu.SMEM)
    hbm = pl.BlockSpec(memory_space=pl.ANY)
    sigma, energy = pl.pallas_call(
        functools.partial(kernel, sectors, ops),
        out_shape=(
            jax.ShapeDtypeStruct((1, rows, width), F32),
            jax.ShapeDtypeStruct((1, 1), F32),
        ),
        in_specs=[smem, smem, vmem, vmem, hbm, hbm],
        out_specs=(vmem, vmem),
        scratch_shapes=[
            operators, operators, operators,
            pltpu.VMEM((sectors, PAIR, far_count, rows, width), BF16),
            full, full,
            pltpu.VMEM((height, terms * width), BF16),
            pltpu.VMEM((height, width), F32),
            block32, block16, block16, block16, block16,
            pltpu.VMEM((sectors, rows, width), F32),
            block32, block16, block16, block16, block16,
            pltpu.VMEM((2, 8, 128), F32),
            pltpu.VMEM((2, 8, 128), F32),
            pltpu.VMEM((far_count, 2, 8, 128), F32),
            pltpu.VMEM((sectors, 2, 8, 128), F32),
            dma((2,)),
            dma((2, far_count)), *[dma((far_count,))] * 3,
            dma((sec_far, PAIR, far_count)), dma((sec_far, PAIR)),
            *[dma((sec_far, PAIR))] * 2,
            *[dma((2, sec_far))] * 2,
            *[dma((2 * far_count,))] * 4,
            *[dma((far_count + sectors,))] * 2,
        ],
        compiler_params=pltpu.CompilerParams(
            collective_id=0, has_side_effects=True, vmem_limit_bytes=56 * 1024 * 1024
        ),
        cost_estimate=pl.CostEstimate(
            flops=8 * terms * height * height * width,
            bytes_accessed=4 * terms * height * width,
            transcendentals=0,
        ),
    )(partner, sector_sizes, wavefunction, diagonal, left_ops, right_ops)

    energy = energy[0, 0]
    row_index = lax.axis_index("op") * rows + jnp.arange(rows, dtype=jnp.int32)
    col_index = jnp.arange(width, dtype=jnp.int32)
    live_mask = (row_index[None, :, None] < sector_sizes[:, None, None]) & (
        col_index[None, None, :] < sector_sizes[:, None, None]
    )
    wave = jnp.where(live_mask, wavefunction, jnp.zeros_like(wavefunction)).astype(F32)
    residual = sigma - energy * wave
    updated = wave - residual / jnp.maximum(jnp.abs(diagonal - energy), 1.0)
    return (updated, residual)


def solution(mesh):
    return jax.shard_map(
        functools.partial(per_device, mesh.shape["sec"], mesh.shape["op"]),
        mesh=mesh,
        in_specs=(
            P("sec", "op", None),
            P("sec", "op", None, None),
            P("sec", "op", None, None),
            P("sec", "op", None),
            P("sec"),
            P(),
        ),
        out_specs=(P("sec", "op", None), P("sec", "op", None)),
        check_vma=False,
    )
```

```python
import functools

import jax
import jax.numpy as jnp
from jax import lax
from jax.experimental import pallas as pl
from jax.experimental.pallas import tpu as pltpu
from jax.sharding import PartitionSpec as P

MESH = pl.DeviceIdType.MESH
F32 = jnp.float32
BF16 = jnp.bfloat16
PAIR = 2


def nt_dot(a, b):
    return lax.dot_general(a, b, (((1,), (1,)), ((), ())), preferred_element_type=F32)


def nn_dot(a, b):
    return lax.dot_general(a, b, (((1,), (0,)), ((), ())), preferred_element_type=F32)


def fold_sum(value):
    rows, width = value.shape
    part = jnp.sum(value.reshape(rows // 8, 8, width), axis=0)
    total = part[:, :128]
    for start in range(128, width, 128):
        total = total + part[:, start : start + 128]
    return total


def kernel(
    sectors, ops,
    partner_ref, sizes_ref, wave_ref, diag_ref, left_hbm, right_hbm,
    sigma_ref, energy_ref,
    left, right, left_t, blocks, own_full, other_full, lhs, inner, acc,
    adj_keep, adj_ys, adj_yr, adj_zs, adj_zr, routed,
    dir_keep, dir_ys, dir_yr, dir_zs, dir_zr,
    scalars, scalar_y, scalar_z, scalar_s,
    load_sem,
    chain_send, chain_recv, near_send, near_recv,
    sec_send, sec_recv, mate_send, mate_recv, route_send, route_recv,
    adj_send, adj_recv, dir_send, dir_recv, sc_send, sc_recv,
):
    far_count = ops // PAIR
    sec_far = sectors // PAIR
    me_sec = lax.axis_index("sec")
    me_op = lax.axis_index("op")
    far, near = me_op // PAIR, lax.rem(me_op, PAIR)
    chip, core = me_sec // PAIR, lax.rem(me_sec, PAIR)
    rows, width = wave_ref.shape[1:]
    terms = left.shape[0]

    def far_at(step):
        return lax.rem(far + step + far_count, far_count)

    def sec_at(step):
        return lax.rem(me_sec + step + sectors, sectors)

    def chip_at(step):
        return lax.rem(chip + step + sec_far, sec_far) * PAIR

    near_peer = (me_sec, far * PAIR + (1 - near))
    up_peer = (me_sec, me_op + PAIR)
    down_peer = (me_sec, me_op - PAIR)
    mate = (chip * PAIR + (1 - core), me_op)

    def far_peer(step):
        return (me_sec, far_at(step) * PAIR + near)

    def sec_peer(step):
        return (sec_at(step), me_op)

    def chip_peer(step):
        return (chip_at(step) + core, me_op)

    def remote(src, dst, send, recv, device):
        return pltpu.make_async_remote_copy(
            src_ref=src, dst_ref=dst, send_sem=send, recv_sem=recv, device_id=device, device_id_type=MESH
        )

    started = []

    def send(*args):
        remote(*args).start()
        started.append((None, args))

    def send_if(cond, *args):
        @pl.when(cond)
        def _():
            remote(*args).start()

        started.append((cond, args))

    def recv(dst, send_sem, recv_sem):
        remote(dst, dst, send_sem, recv_sem, near_peer).wait_recv()

    load_left = pltpu.make_async_copy(left_hbm.at[0], left, load_sem.at[0])
    load_right = pltpu.make_async_copy(right_hbm.at[0], right, load_sem.at[1])
    load_left.start()
    load_right.start()

    barrier = pltpu.get_barrier_semaphore()
    peers = [near_peer]
    peers += [far_peer(step) for step in range(1, far_count)]
    peers += [sec_peer(step) for step in range(1, sectors)]
    for peer in peers:
        pl.semaphore_signal(barrier, inc=1, device_id=peer, device_id_type=MESH)

    size = sizes_ref[0]
    row_index = me_op * rows + lax.broadcasted_iota(jnp.int32, (rows, width), 0)
    col_index = lax.broadcasted_iota(jnp.int32, (rows, width), 1)
    live_mask = (row_index < size) & (col_index < size)
    wave = jnp.where(live_mask, wave_ref[0].astype(F32), 0.0)
    blocks[me_sec, near, far] = wave.astype(BF16)
    diag = diag_ref[0]
    scalars[0] = fold_sum(diag * wave * wave)
    scalars[1] = fold_sum(wave * wave)
    pl.semaphore_wait(barrier, len(peers))

    has_up, has_down = far + 1 < far_count, far > 0

    def to_chips(cond, half, place):
        block = blocks.at[me_sec, half, place]
        for step in range(1, sec_far):
            args = (block, block, sec_send.at[step, half, place], sec_recv.at[step, half], chip_peer(step))
            send(*args) if cond is None else send_if(cond, *args)

    mine = blocks.at[me_sec, near, far]
    send_if(has_up, mine, mine, chain_send.at[0, far], chain_recv.at[far], up_peer)
    send_if(has_down, mine, mine, chain_send.at[1, far], chain_recv.at[far], down_peer)
    send(mine, mine, near_send.at[far], near_recv.at[far], near_peer)
    to_chips(None, near, far)

    def arrive(cond, place, onward, way, peer):
        block = blocks.at[me_sec, near, place]

        @pl.when(cond)
        def _():
            recv(block, chain_send.at[way, place], chain_recv.at[place])

        send_if(cond & onward, block, block, chain_send.at[way, place], chain_recv.at[place], peer)
        send_if(cond, block, block, near_send.at[place], near_recv.at[place], near_peer)
        to_chips(cond, near, place)

    load_left.wait()

    def turn(term, carry):
        left_t[term] = left[term].T
        return carry

    turned = 0
    for step in range(1, far_count):
        if turned < terms:
            turn(turned, 0)
            turned += 1
        arrive(far - step >= 0, jnp.maximum(far - step, 0), has_up, 0, up_peer)
        arrive(far + step < far_count, jnp.minimum(far + step, far_count - 1), has_down, 1, down_peer)
    for term in range(turned, terms):
        turn(term, 0)

    def to_mate(sector, step, half):
        part = blocks.at[sector, half]
        send(part, part, mate_send.at[step, half], mate_recv.at[step, half], mate)

    to_mate(me_sec, 0, near)
    for step in range(far_count):
        place = far_at(-step)
        recv(blocks.at[me_sec, 1 - near, place], near_send.at[place], near_recv.at[place])
        to_chips(None, 1 - near, place)
    to_mate(me_sec, 0, 1 - near)

    def assemble(sector, full):
        for place in range(far_count):
            pair = [blocks[sector, half, place] for half in range(PAIR)]
            if rows % 16:
                pair = [part.astype(F32) for part in pair]
            full[place * span : (place + 1) * span, :] = jnp.concatenate(pair, axis=0).astype(BF16)

    span = PAIR * rows
    assemble(me_sec, own_full)
    load_right.wait()

    order = list(range(1, far_count)) + [0]
    half = (far_count + 1) // 2
    groups = [order[:half], order[half:]]

    def place_of(step):
        return pl.ds(pl.multiple_of(far_at(step) * span, span), span)

    tile = 256 if width % 256 == 0 else width

    def tile_at(index):
        return pl.ds(pl.multiple_of(index * tile, tile), tile)

    def adjoint_tile(part, term, columns):
        return nn_dot(part, right[term, :, columns])

    def direct_tile(part, term, columns):
        return nt_dot(part, right[term, columns, :])

    def products(group, base, left_side, middle, last_tile, keep, ys, yr, sends, recvs):
        count = len(group) * span

        def one(term, carry):
            for at, step in enumerate(group):
                lhs[at * span : (at + 1) * span, :] = left_side[term, place_of(step), :]
            for index in range(width // tile):
                columns = slice(index * tile, (index + 1) * tile)
                inner[term, :count, columns] = nn_dot(lhs[:count, :], middle[:, columns]).astype(BF16)
            return carry

        def two(index, carry):
            columns = tile_at(index)
            total = last_tile(inner[0, :count, :], 0, columns)
            for term in range(1, terms):
                total = total + last_tile(inner[term, :count, :], term, columns)
            acc[base : base + count, columns] = total
            return carry

        lax.fori_loop(0, terms, one, 0)
        lax.fori_loop(0, width // tile, two, 0)
        for at, step in enumerate(group):
            start = base + at * span
            first = acc[start : start + rows, :]
            second = acc[start + rows : start + span, :]
            keep[step] = jnp.where(near == 0, first, second)
            ys[step] = jnp.where(near == 0, second, first).astype(BF16)
            send(ys.at[step], yr.at[step], sends.at[step], recvs.at[step], near_peer)

    def inner_product(group, base, weight):
        for at, step in enumerate(group):
            start = base + at * span
            scalars[0] += fold_sum(acc[start : start + span, :] * weight[place_of(step), :].astype(F32))

    def pass_on(step, keep, yr, zs, zr, sends, recvs):
        recv(yr.at[step], sends.at[step], recvs.at[step])
        summed = keep[step] + yr[step].astype(F32)
        if step == 0:
            keep[0] = summed
        else:
            zs[step] = summed.astype(BF16)
            at = far_count + step
            send(zs.at[step], zr.at[step], sends.at[at], recvs.at[at], far_peer(step))

    def finish(keep, zr, sends, recvs):
        total = keep[0]
        for step in range(1, far_count):
            at = far_count + step
            recv(zr.at[step], sends.at[at], recvs.at[at])
            total = total + zr[step].astype(F32)
        return total

    def from_chips(half):
        for step in range(1, sec_far):
            sector = chip_at(-step) + core
            recv(blocks.at[sector, half], sec_send.at[step, half, 0], sec_recv.at[step, half])
            to_mate(sector, step, half)

    adj = (adj_keep, adj_ys, adj_yr, adj_send, adj_recv)
    direct = (dir_keep, dir_ys, dir_yr, dir_send, dir_recv)
    adj_pass = (adj_keep, adj_yr, adj_zs, adj_zr, adj_send, adj_recv)
    dir_pass = (dir_keep, dir_yr, dir_zs, dir_zr, dir_send, dir_recv)
    second_base = len(groups[0]) * span

    products(groups[0], 0, left_t, own_full, adjoint_tile, *adj)
    from_chips(near)
    products(groups[1], second_base, left_t, own_full, adjoint_tile, *adj)
    for step in groups[0]:
        pass_on(step, *adj_pass)
    from_chips(1 - near)
    for step in range(sec_far):
        sector = chip_at(-step) + (1 - core)
        for side in (near, 1 - near):
            recv(blocks.at[sector, side], mate_send.at[step, side], mate_recv.at[step, side])
    assemble(partner_ref[me_sec], other_full)
    inner_product(groups[0], 0, other_full)
    inner_product(groups[1], second_base, other_full)

    products(groups[0], 0, left, other_full, direct_tile, *direct)
    for step in groups[1]:
        pass_on(step, *adj_pass)
    products(groups[1], second_base, left, other_full, direct_tile, *direct)
    for step in groups[0]:
        pass_on(step, *dir_pass)
    inner_product(groups[0], 0, own_full)
    inner_product(groups[1], second_base, own_full)

    send(scalars, scalar_y, sc_send.at[0], sc_recv.at[0], near_peer)
    routed[me_sec] = finish(adj_keep, adj_zr, adj_send, adj_recv)
    rows_out = routed.at[me_sec]
    for step in range(1, sec_far):
        send(rows_out, rows_out, route_send.at[0, step], route_recv.at[0, step], chip_peer(step))
    send(rows_out, rows_out, route_send.at[1, 0], route_recv.at[1, 0], mate)
    recv(scalar_y, sc_send.at[0], sc_recv.at[0])
    scalar_z[0] = scalars[...] + scalar_y[...]
    for step in range(1, far_count):
        send(scalar_z.at[0], scalar_z.at[step], sc_send.at[step], sc_recv.at[step], far_peer(step))
    for step in groups[1]:
        pass_on(step, *dir_pass)

    inner_sum = scalar_z[0]
    for step in range(1, far_count):
        recv(scalar_z.at[step], sc_send.at[step], sc_recv.at[step])
        inner_sum = inner_sum + scalar_z[step]
    scalar_s[0] = inner_sum
    for step in range(1, sectors):
        at = far_count + step
        send(scalar_s.at[0], scalar_s.at[step], sc_send.at[at], sc_recv.at[at], sec_peer(step))
    for step in range(1, sec_far):
        part = routed.at[chip_at(-step) + core]
        recv(part, route_send.at[0, step], route_recv.at[0, step])
        send(part, part, route_send.at[1, step], route_recv.at[1, step], mate)
    for step in range(1, sectors):
        at = far_count + step
        recv(scalar_s.at[step], sc_send.at[at], sc_recv.at[at])
        inner_sum = inner_sum + scalar_s[step]
    energy_ref[...] = jnp.sum(inner_sum[0], keepdims=True) / jnp.sum(inner_sum[1], keepdims=True)

    source = jnp.int32(0)
    for sector in range(sectors):
        source = jnp.where(partner_ref[sector] == me_sec, sector, source)
    for step in range(sec_far):
        recv(routed.at[chip_at(-step) + (1 - core)], route_send.at[1, step], route_recv.at[1, step])
    other_part = routed[source] + diag_ref[0] * wave
    direct_part = finish(dir_keep, dir_zr, dir_send, dir_recv)
    sigma_ref[0] = jnp.where(live_mask, direct_part + other_part, 0.0)

    for cond, args in started:
        if cond is None:
            remote(*args).wait_send()
        else:

            @pl.when(cond)
            def _():
                remote(*args).wait_send()


def per_device(sectors, ops, wavefunction, left_ops, right_ops, diagonal, sector_sizes, partner):
    _, rows, width = wavefunction.shape
    terms, height = left_ops.shape[1:3]
    far_count = ops // PAIR
    block16 = pltpu.VMEM((far_count, rows, width), BF16)
    block32 = pltpu.VMEM((far_count, rows, width), F32)
    sec_far = sectors // PAIR
    full = pltpu.VMEM((height, width), BF16)
    operators = pltpu.VMEM((terms, height, width), BF16)
    dma = pltpu.SemaphoreType.DMA
    vmem = pl.BlockSpec(memory_space=pltpu.VMEM)
    smem = pl.BlockSpec(memory_space=pltpu.SMEM)
    hbm = pl.BlockSpec(memory_space=pl.ANY)
    sigma, energy = pl.pallas_call(
        functools.partial(kernel, sectors, ops),
        out_shape=(
            jax.ShapeDtypeStruct((1, rows, width), F32),
            jax.ShapeDtypeStruct((1, 1), F32),
        ),
        in_specs=[smem, smem, vmem, vmem, hbm, hbm],
        out_specs=(vmem, vmem),
        scratch_shapes=[
            operators, operators, operators,
            pltpu.VMEM((sectors, PAIR, far_count, rows, width), BF16),
            full, full, full, operators,
            pltpu.VMEM((height, width), F32),
            block32, block16, block16, block16, block16,
            pltpu.VMEM((sectors, rows, width), F32),
            block32, block16, block16, block16, block16,
            pltpu.VMEM((2, 8, 128), F32),
            pltpu.VMEM((2, 8, 128), F32),
            pltpu.VMEM((far_count, 2, 8, 128), F32),
            pltpu.VMEM((sectors, 2, 8, 128), F32),
            dma((2,)),
            dma((2, far_count)), *[dma((far_count,))] * 3,
            dma((sec_far, PAIR, far_count)), dma((sec_far, PAIR)),
            *[dma((sec_far, PAIR))] * 2,
            *[dma((2, sec_far))] * 2,
            *[dma((2 * far_count,))] * 4,
            *[dma((far_count + sectors,))] * 2,
        ],
        compiler_params=pltpu.CompilerParams(
            collective_id=0, has_side_effects=True, vmem_limit_bytes=56 * 1024 * 1024
        ),
        cost_estimate=pl.CostEstimate(
            flops=8 * terms * height * height * width,
            bytes_accessed=4 * terms * height * width,
            transcendentals=0,
        ),
    )(partner, sector_sizes, wavefunction, diagonal, left_ops, right_ops)

    energy = energy[0, 0]
    row_index = lax.axis_index("op") * rows + jnp.arange(rows, dtype=jnp.int32)
    col_index = jnp.arange(width, dtype=jnp.int32)
    live_mask = (row_index[None, :, None] < sector_sizes[:, None, None]) & (
        col_index[None, None, :] < sector_sizes[:, None, None]
    )
    wave = jnp.where(live_mask, wavefunction, jnp.zeros_like(wavefunction)).astype(F32)
    residual = sigma - energy * wave
    updated = wave - residual / jnp.maximum(jnp.abs(diagonal - energy), 1.0)
    return (updated, residual)


def solution(mesh):
    return jax.shard_map(
        functools.partial(per_device, mesh.shape["sec"], mesh.shape["op"]),
        mesh=mesh,
        in_specs=(
            P("sec", "op", None),
            P("sec", "op", None, None),
            P("sec", "op", None, None),
            P("sec", "op", None),
            P("sec"),
            P(),
        ),
        out_specs=(P("sec", "op", None), P("sec", "op", None)),
        check_vma=False,
    )
```

```python
import functools

import jax
import jax.numpy as jnp
from jax import lax
from jax.experimental import pallas as pl
from jax.experimental.pallas import tpu as pltpu
from jax.sharding import PartitionSpec as P

MESH = pl.DeviceIdType.MESH
F32 = jnp.float32
BF16 = jnp.bfloat16
PAIR = 2


def nt_dot(a, b):
    return lax.dot_general(a, b, (((1,), (1,)), ((), ())), preferred_element_type=F32)


def nn_dot(a, b):
    return lax.dot_general(a, b, (((1,), (0,)), ((), ())), preferred_element_type=F32)


def fold_sum(value):
    rows, width = value.shape
    part = jnp.sum(value.reshape(rows // 8, 8, width), axis=0)
    total = part[:, :128]
    for start in range(128, width, 128):
        total = total + part[:, start : start + 128]
    return total


def kernel(
    sectors, ops,
    partner_ref, sizes_ref, wave_ref, diag_ref, left_hbm, right_hbm,
    sigma_ref, energy_ref,
    left, right, left_t, blocks, own_full, other_full, lhs, inner, adj_acc, dir_acc,
    adj_keep, adj_ys, adj_yr, adj_zs, adj_zr, routed,
    dir_keep, dir_ys, dir_yr, dir_zs, dir_zr,
    scalars, scalar_y, scalar_z, scalar_s,
    load_sem,
    chain_send, chain_recv, near_send, near_recv,
    sec_send, sec_recv, mate_send, mate_recv, route_send, route_recv,
    adj_send, adj_recv, dir_send, dir_recv, sc_send, sc_recv,
):
    far_count = ops // PAIR
    sec_far = sectors // PAIR
    me_sec = lax.axis_index("sec")
    me_op = lax.axis_index("op")
    far, near = me_op // PAIR, lax.rem(me_op, PAIR)
    chip, core = me_sec // PAIR, lax.rem(me_sec, PAIR)
    rows, width = wave_ref.shape[1:]
    terms = left.shape[0]

    def far_at(step):
        return lax.rem(far + step + far_count, far_count)

    def sec_at(step):
        return lax.rem(me_sec + step + sectors, sectors)

    def chip_at(step):
        return lax.rem(chip + step + sec_far, sec_far) * PAIR

    near_peer = (me_sec, far * PAIR + (1 - near))
    up_peer = (me_sec, me_op + PAIR)
    down_peer = (me_sec, me_op - PAIR)
    mate = (chip * PAIR + (1 - core), me_op)

    def far_peer(step):
        return (me_sec, far_at(step) * PAIR + near)

    def sec_peer(step):
        return (sec_at(step), me_op)

    def chip_peer(step):
        return (chip_at(step) + core, me_op)

    def remote(src, dst, send, recv, device):
        return pltpu.make_async_remote_copy(
            src_ref=src, dst_ref=dst, send_sem=send, recv_sem=recv, device_id=device, device_id_type=MESH
        )

    started = []

    def send(*args):
        remote(*args).start()
        started.append((None, args))

    def send_if(cond, *args):
        @pl.when(cond)
        def _():
            remote(*args).start()

        started.append((cond, args))

    def recv(dst, send_sem, recv_sem):
        remote(dst, dst, send_sem, recv_sem, near_peer).wait_recv()

    load_left = pltpu.make_async_copy(left_hbm.at[0], left, load_sem.at[0])
    load_right = pltpu.make_async_copy(right_hbm.at[0], right, load_sem.at[1])
    load_left.start()
    load_right.start()

    barrier = pltpu.get_barrier_semaphore()
    peers = [near_peer]
    peers += [far_peer(step) for step in range(1, far_count)]
    peers += [sec_peer(step) for step in range(1, sectors)]
    for peer in peers:
        pl.semaphore_signal(barrier, inc=1, device_id=peer, device_id_type=MESH)

    size = sizes_ref[0]
    row_index = me_op * rows + lax.broadcasted_iota(jnp.int32, (rows, width), 0)
    col_index = lax.broadcasted_iota(jnp.int32, (rows, width), 1)
    live_mask = (row_index < size) & (col_index < size)
    wave = jnp.where(live_mask, wave_ref[0].astype(F32), 0.0)
    blocks[me_sec, near, far] = wave.astype(BF16)
    diag = diag_ref[0]
    scalars[0] = fold_sum(diag * wave * wave)
    scalars[1] = fold_sum(wave * wave)
    pl.semaphore_wait(barrier, len(peers))

    has_up, has_down = far + 1 < far_count, far > 0

    def to_chips(cond, half, place):
        block = blocks.at[me_sec, half, place]
        for step in range(1, sec_far):
            args = (block, block, sec_send.at[step, half, place], sec_recv.at[step, half], chip_peer(step))
            send(*args) if cond is None else send_if(cond, *args)

    mine = blocks.at[me_sec, near, far]
    send_if(has_up, mine, mine, chain_send.at[0, far], chain_recv.at[far], up_peer)
    send_if(has_down, mine, mine, chain_send.at[1, far], chain_recv.at[far], down_peer)
    send(mine, mine, near_send.at[far], near_recv.at[far], near_peer)
    to_chips(None, near, far)

    def arrive(cond, place, onward, way, peer):
        block = blocks.at[me_sec, near, place]

        @pl.when(cond)
        def _():
            recv(block, chain_send.at[way, place], chain_recv.at[place])

        send_if(cond & onward, block, block, chain_send.at[way, place], chain_recv.at[place], peer)
        send_if(cond, block, block, near_send.at[place], near_recv.at[place], near_peer)
        to_chips(cond, near, place)

    load_left.wait()

    def turn(term, carry):
        left_t[term] = left[term].T
        return carry

    turned = 0
    for step in range(1, far_count):
        if turned < terms:
            turn(turned, 0)
            turned += 1
        arrive(far - step >= 0, jnp.maximum(far - step, 0), has_up, 0, up_peer)
        arrive(far + step < far_count, jnp.minimum(far + step, far_count - 1), has_down, 1, down_peer)
    for term in range(turned, terms):
        turn(term, 0)

    def to_mate(sector, step, half):
        part = blocks.at[sector, half]
        send(part, part, mate_send.at[step, half], mate_recv.at[step, half], mate)

    to_mate(me_sec, 0, near)
    for step in range(far_count):
        place = far_at(-step)
        recv(blocks.at[me_sec, 1 - near, place], near_send.at[place], near_recv.at[place])
        to_chips(None, 1 - near, place)
    to_mate(me_sec, 0, 1 - near)

    def assemble(sector, full):
        for place in range(far_count):
            pair = [blocks[sector, half, place] for half in range(PAIR)]
            if rows % 16:
                pair = [part.astype(F32) for part in pair]
            full[place * span : (place + 1) * span, :] = jnp.concatenate(pair, axis=0).astype(BF16)

    span = PAIR * rows
    assemble(me_sec, own_full)
    load_right.wait()

    order = list(range(1, far_count)) + [0]
    quarter = max(far_count // 4, 1)
    groups = [order[:quarter], order[quarter:-quarter], order[-quarter:]]
    bases = [0, quarter * span, (far_count - quarter) * span]

    def place_of(step):
        return pl.ds(pl.multiple_of(far_at(step) * span, span), span)

    tile = 256 if width % 256 == 0 else width

    def tile_at(index):
        return pl.ds(pl.multiple_of(index * tile, tile), tile)

    def adjoint_tile(part, term, columns):
        return nn_dot(part, right[term, :, columns])

    def direct_tile(part, term, columns):
        return nt_dot(part, right[term, columns, :])

    def products(which, left_side, middle, last_tile, acc, keep, ys, yr, sends, recvs):
        group, base = groups[which], bases[which]
        count = len(group) * span

        def one(term, carry):
            for at, step in enumerate(group):
                lhs[at * span : (at + 1) * span, :] = left_side[term, place_of(step), :]
            for index in range(width // tile):
                columns = slice(index * tile, (index + 1) * tile)
                inner[term, :count, columns] = nn_dot(lhs[:count, :], middle[:, columns]).astype(BF16)
            return carry

        def two(index, carry):
            columns = tile_at(index)
            total = last_tile(inner[0, :count, :], 0, columns)
            for term in range(1, terms):
                total = total + last_tile(inner[term, :count, :], term, columns)
            acc[base : base + count, columns] = total
            return carry

        lax.fori_loop(0, terms, one, 0)
        lax.fori_loop(0, width // tile, two, 0)
        for at, step in enumerate(group):
            start = base + at * span
            first = acc[start : start + rows, :]
            second = acc[start + rows : start + span, :]
            keep[step] = jnp.where(near == 0, first, second)
            ys[step] = jnp.where(near == 0, second, first).astype(BF16)
            send(ys.at[step], yr.at[step], sends.at[step], recvs.at[step], near_peer)

    def inner_product(which, acc, weight):
        for at, step in enumerate(groups[which]):
            start = bases[which] + at * span
            scalars[0] += fold_sum(acc[start : start + span, :] * weight[place_of(step), :].astype(F32))

    def pass_on(step, keep, yr, zs, zr, sends, recvs):
        recv(yr.at[step], sends.at[step], recvs.at[step])
        summed = keep[step] + yr[step].astype(F32)
        if step == 0:
            keep[0] = summed
        else:
            zs[step] = summed.astype(BF16)
            at = far_count + step
            send(zs.at[step], zr.at[step], sends.at[at], recvs.at[at], far_peer(step))

    def finish(keep, zr, sends, recvs):
        total = keep[0]
        for step in range(1, far_count):
            at = far_count + step
            recv(zr.at[step], sends.at[at], recvs.at[at])
            total = total + zr[step].astype(F32)
        return total

    def from_chips(half):
        for step in range(1, sec_far):
            sector = chip_at(-step) + core
            recv(blocks.at[sector, half], sec_send.at[step, half, 0], sec_recv.at[step, half])
            to_mate(sector, step, half)

    adj = (adj_acc, adj_keep, adj_ys, adj_yr, adj_send, adj_recv)
    direct = (dir_acc, dir_keep, dir_ys, dir_yr, dir_send, dir_recv)
    adj_pass = (adj_keep, adj_yr, adj_zs, adj_zr, adj_send, adj_recv)
    dir_pass = (dir_keep, dir_yr, dir_zs, dir_zr, dir_send, dir_recv)

    products(0, left_t, own_full, adjoint_tile, *adj)
    from_chips(near)
    products(1, left_t, own_full, adjoint_tile, *adj)
    for step in groups[0]:
        pass_on(step, *adj_pass)
    products(2, left_t, own_full, adjoint_tile, *adj)
    from_chips(1 - near)
    for step in groups[1]:
        pass_on(step, *adj_pass)
    for step in range(sec_far):
        sector = chip_at(-step) + (1 - core)
        for side in (near, 1 - near):
            recv(blocks.at[sector, side], mate_send.at[step, side], mate_recv.at[step, side])
    assemble(partner_ref[me_sec], other_full)

    products(0, left, other_full, direct_tile, *direct)
    for step in groups[2]:
        pass_on(step, *adj_pass)
    products(1, left, other_full, direct_tile, *direct)
    for step in groups[0]:
        pass_on(step, *dir_pass)
    products(2, left, other_full, direct_tile, *direct)
    for which in range(3):
        inner_product(which, adj_acc, other_full)
        inner_product(which, dir_acc, own_full)

    send(scalars, scalar_y, sc_send.at[0], sc_recv.at[0], near_peer)
    routed[me_sec] = finish(adj_keep, adj_zr, adj_send, adj_recv)
    rows_out = routed.at[me_sec]
    for step in range(1, sec_far):
        send(rows_out, rows_out, route_send.at[0, step], route_recv.at[0, step], chip_peer(step))
    send(rows_out, rows_out, route_send.at[1, 0], route_recv.at[1, 0], mate)
    recv(scalar_y, sc_send.at[0], sc_recv.at[0])
    scalar_z[0] = scalars[...] + scalar_y[...]
    for step in range(1, far_count):
        send(scalar_z.at[0], scalar_z.at[step], sc_send.at[step], sc_recv.at[step], far_peer(step))
    for step in groups[1] + groups[2]:
        pass_on(step, *dir_pass)

    inner_sum = scalar_z[0]
    for step in range(1, far_count):
        recv(scalar_z.at[step], sc_send.at[step], sc_recv.at[step])
        inner_sum = inner_sum + scalar_z[step]
    scalar_s[0] = inner_sum
    for step in range(1, sectors):
        at = far_count + step
        send(scalar_s.at[0], scalar_s.at[step], sc_send.at[at], sc_recv.at[at], sec_peer(step))
    for step in range(1, sec_far):
        part = routed.at[chip_at(-step) + core]
        recv(part, route_send.at[0, step], route_recv.at[0, step])
        send(part, part, route_send.at[1, step], route_recv.at[1, step], mate)
    for step in range(1, sectors):
        at = far_count + step
        recv(scalar_s.at[step], sc_send.at[at], sc_recv.at[at])
        inner_sum = inner_sum + scalar_s[step]
    energy_ref[...] = jnp.sum(inner_sum[0], keepdims=True) / jnp.sum(inner_sum[1], keepdims=True)

    source = jnp.int32(0)
    for sector in range(sectors):
        source = jnp.where(partner_ref[sector] == me_sec, sector, source)
    for step in range(sec_far):
        recv(routed.at[chip_at(-step) + (1 - core)], route_send.at[1, step], route_recv.at[1, step])
    other_part = routed[source] + diag_ref[0] * wave
    direct_part = finish(dir_keep, dir_zr, dir_send, dir_recv)
    sigma_ref[0] = jnp.where(live_mask, direct_part + other_part, 0.0)

    for cond, args in started:
        if cond is None:
            remote(*args).wait_send()
        else:

            @pl.when(cond)
            def _():
                remote(*args).wait_send()


def per_device(sectors, ops, wavefunction, left_ops, right_ops, diagonal, sector_sizes, partner):
    _, rows, width = wavefunction.shape
    terms, height = left_ops.shape[1:3]
    far_count = ops // PAIR
    block16 = pltpu.VMEM((far_count, rows, width), BF16)
    block32 = pltpu.VMEM((far_count, rows, width), F32)
    sec_far = sectors // PAIR
    full = pltpu.VMEM((height, width), BF16)
    operators = pltpu.VMEM((terms, height, width), BF16)
    dma = pltpu.SemaphoreType.DMA
    vmem = pl.BlockSpec(memory_space=pltpu.VMEM)
    smem = pl.BlockSpec(memory_space=pltpu.SMEM)
    hbm = pl.BlockSpec(memory_space=pl.ANY)
    sigma, energy = pl.pallas_call(
        functools.partial(kernel, sectors, ops),
        out_shape=(
            jax.ShapeDtypeStruct((1, rows, width), F32),
            jax.ShapeDtypeStruct((1, 1), F32),
        ),
        in_specs=[smem, smem, vmem, vmem, hbm, hbm],
        out_specs=(vmem, vmem),
        scratch_shapes=[
            operators, operators, operators,
            pltpu.VMEM((sectors, PAIR, far_count, rows, width), BF16),
            full, full, full, operators,
            *[pltpu.VMEM((height, width), F32)] * 2,
            block32, block16, block16, block16, block16,
            pltpu.VMEM((sectors, rows, width), F32),
            block32, block16, block16, block16, block16,
            pltpu.VMEM((2, 8, 128), F32),
            pltpu.VMEM((2, 8, 128), F32),
            pltpu.VMEM((far_count, 2, 8, 128), F32),
            pltpu.VMEM((sectors, 2, 8, 128), F32),
            dma((2,)),
            dma((2, far_count)), *[dma((far_count,))] * 3,
            dma((sec_far, PAIR, far_count)), dma((sec_far, PAIR)),
            *[dma((sec_far, PAIR))] * 2,
            *[dma((2, sec_far))] * 2,
            *[dma((2 * far_count,))] * 4,
            *[dma((far_count + sectors,))] * 2,
        ],
        compiler_params=pltpu.CompilerParams(
            collective_id=0, has_side_effects=True, vmem_limit_bytes=56 * 1024 * 1024
        ),
        cost_estimate=pl.CostEstimate(
            flops=8 * terms * height * height * width,
            bytes_accessed=4 * terms * height * width,
            transcendentals=0,
        ),
    )(partner, sector_sizes, wavefunction, diagonal, left_ops, right_ops)

    energy = energy[0, 0]
    row_index = lax.axis_index("op") * rows + jnp.arange(rows, dtype=jnp.int32)
    col_index = jnp.arange(width, dtype=jnp.int32)
    live_mask = (row_index[None, :, None] < sector_sizes[:, None, None]) & (
        col_index[None, None, :] < sector_sizes[:, None, None]
    )
    wave = jnp.where(live_mask, wavefunction, jnp.zeros_like(wavefunction)).astype(F32)
    residual = sigma - energy * wave
    updated = wave - residual / jnp.maximum(jnp.abs(diagonal - energy), 1.0)
    return (updated, residual)


def solution(mesh):
    return jax.shard_map(
        functools.partial(per_device, mesh.shape["sec"], mesh.shape["op"]),
        mesh=mesh,
        in_specs=(
            P("sec", "op", None),
            P("sec", "op", None, None),
            P("sec", "op", None, None),
            P("sec", "op", None),
            P("sec"),
            P(),
        ),
        out_specs=(P("sec", "op", None), P("sec", "op", None)),
        check_vma=False,
    )
```
